32 devices in a mesh: dp: 4 (over z), seq: 8 (over y, x, core).
Axes of the slice: x: 2, y: 2, z: 4, core: 2. Of those that a mesh axis runs over, the one named last changes fastest.
Arguments:
- hidden: bfloat16 [4096, 5120], P(('dp', 'seq')), may hold values from -6 to 6
- queries: bfloat16 [4096, 4096], P(('dp', 'seq')), may hold values from -330 to 330
- key_states: bfloat16 [4096, 4096], P(('dp', 'seq')), may hold values from -18 to 18
- value_states: bfloat16 [4096, 4096], P(('dp', 'seq')), may hold values from -6 to 6
- attention_out: bfloat16 [4096, 4096], P(('dp', 'seq')), may hold values from -6 to 6
- grad_out: bfloat16 [4096, 4096], P(('dp', 'seq')), may hold values from -6 to 6
- lengths: int32 [4, 4], P('dp'), may hold values from 1 to 512, 1024 in all within a row
- down_query: bfloat16 [8, 5120], replicated, may hold values from -0.0012207031 to 0.0012207031
- up_query: bfloat16 [8, 4096], replicated, may hold values from -0.0014648438 to 0.0014648438
- down_value: bfloat16 [8, 5120], replicated, may hold values from -0.0012207031 to 0.0012207031
- up_value: bfloat16 [8, 4096], replicated, may hold values from -0.0014648438 to 0.0014648438
Outputs:
- grad_queries: bfloat16 [4096, 4096], P(('dp', 'seq'))
- grad_keys: bfloat16 [4096, 4096], P(('dp', 'seq'))
- value_gradients: bfloat16 [4096, 4096], P(('dp', 'seq'))
- query_down_gradient: float32 [8, 5120], P(None, 'dp')
- query_up_gradient: float32 [8, 4096], P(None, 'dp')
- value_down_gradient: float32 [8, 5120], P(None, 'dp')
- value_up_gradient: float32 [8, 4096], P(None, 'dp')
The draws below stay inside these ranges and needn't reach their ends.
Inputs may be any that keep to these rules, and one draw needn't show every extreme that they name: Each row lists the lengths of the 4 sequences of one pack in packing order; a row sums to 1024.
All inputs are finite; a program needn't handle non-finite values.
Results may differ from the reference program's by a relative error of at most 0.0067.
Values may be sent and summed in bfloat16 or wider, within the bound.
No kernel may reach another device: no remote copies, remote signals or barrier semaphores. Data moves between devices by JAX's collectives and lax.ppermute only.
A program may use at most 64 MiB of HBM per device.

```python
import math
import jax
import jax.numpy as jnp
import numpy as np
from jax import lax

D = 5120
H = 32
HD = 128
ADAPTER_RANK = 8
ADAPTER_ALPHA = 16
NSEQ = 4
S = 1024
TOKENS = 4096
HH = 4096
N_DP = 4


def query_key_pair(key):
    base_key = jax.random.fold_in(key, 7)
    key_query, key_keys = jax.random.split(base_key, 2)
    queries = jnp.clip(jax.random.normal(key_query, (TOKENS, HH), jnp.float32), -6.0, 6.0)
    keys_drawn = jnp.clip(jax.random.normal(key_keys, (TOKENS, HH), jnp.float32), -6.0, 6.0)
    return (queries, keys_drawn)


def draw_queries(key, part):
    return query_key_pair(key)[0].astype(jnp.bfloat16)


def draw_key_states(key, part):
    return query_key_pair(key)[1].astype(jnp.bfloat16)


def spiked(entries, rng, source, target, blocks, factor):
    owner, partner = [(jnp.arange(entries.shape[position]) // (entries.shape[position] // blocks)).reshape([-1 if axis == position else 1 for axis in range(entries.ndim)]) for position in (source, target)]
    chosen = jax.random.permutation(rng, blocks)[partner]
    strong = (owner == chosen) | (owner == (partner + blocks // 2) % blocks)
    return jnp.where(strong, factor * entries, entries)


def steps_of(stream_key, shape, cuts, smallest, high):
    def one(axis_at, parts):
        heights = jax.random.uniform(jax.random.fold_in(jax.random.fold_in(stream_key, 6), axis_at), (parts,), jnp.float32, smallest / len(cuts), high / len(cuts))
        return jnp.repeat(jnp.exp(heights), shape[axis_at] // parts).reshape((-1,) + (1,) * (len(shape) - axis_at - 1))

    level = one(*cuts[0])
    for cut in cuts[1:]:
        level = level * one(*cut)
    return level


def split_up(number_of, total, reach, lean):
    loads = [(1 << 20) // math.isqrt(standing ** lean) + 1 for standing in range(2, number_of + 1)]
    spare, given = total - reach - (number_of - 1), [1] * (number_of - 1)
    while spare > 0:
        free = [i for i in range(number_of - 1) if given[i] < reach]
        mass, budget = sum([loads[i] for i in free]), spare
        for i in free:
            extra = min(reach - given[i], max(1, budget * loads[i] // mass), spare)
            given[i] = given[i] + extra
            spare = spare - extra
    return np.array([reach] + given)


def ragged(own_key, number_of, total, reach, lean):
    if number_of == 2:
        one = jax.random.randint(own_key, (), max(1, total - reach), min(reach, total - 1) + 1)
        return jnp.stack([one, total - one])
    sizes = jnp.asarray(split_up(number_of, total, reach, lean), jnp.int32)
    twos = (number_of - 1) // 2
    source_of, sink = sizes[1:1 + 2 * twos:2], sizes[2:2 + 2 * twos:2]
    room = jnp.minimum(source_of - 1, reach - sink)
    shifted = jax.random.randint(jax.random.fold_in(own_key, 1), (twos,), 0, 1 << 20) % (room + 1)
    sizes = sizes.at[1:1 + 2 * twos:2].set(source_of - shifted).at[2:2 + 2 * twos:2].set(sink + shifted)
    return sizes[jax.random.permutation(jax.random.fold_in(own_key, 2), number_of)]


def gaussian(rng, dims, scale, most, cuts=(), kind=jnp.bfloat16):
    loudness = steps_of(rng, dims, cuts, -0.22, 0.18) if cuts else 1.0
    values = jax.random.normal(rng, dims, jnp.float32) * scale * loudness
    return jnp.minimum(jnp.maximum(values, -most), most).astype(kind)


def noise_with(rng, extent, width, most, pieces, heavy, kind=jnp.bfloat16):
    entries = width * jax.random.normal(rng, extent, jnp.float32)
    if pieces:
        entries = entries * steps_of(rng, extent, pieces, -0.22, 0.18)
    return jnp.clip(spiked(entries, jax.random.fold_in(rng, 3), *heavy), -most, most).astype(kind)


def setup_inputs(seed: int = 0) -> dict:
    key_of = jax.random.split(jax.random.key(seed), 12)
    hidden = noise_with(key_of[0], (TOKENS, D), 1.0, 6.0, ((0, 32),), (0, 1, 32, 2.75))
    queries = draw_queries(jax.random.fold_in(key_of[11], 71), 0)
    key_states = draw_key_states(jax.random.fold_in(key_of[11], 71), 0)
    value_states = gaussian(key_of[3], (TOKENS, HH), 1.0, 6.0, ((0, 32),))
    attention_out = gaussian(key_of[4], (TOKENS, HH), 1.0, 6.0, ((0, 32),))
    grad_out = noise_with(key_of[5], (TOKENS, HH), 1.0, 6.0, ((0, 32),), (0, 1, 32, 2.75))
    lengths = jax.vmap(lambda own: ragged(own, NSEQ, S, S // 2, 2))(jax.random.split(key_of[6], N_DP)).reshape((N_DP, NSEQ)).astype(jnp.int32)
    down_query = gaussian(key_of[7], (ADAPTER_RANK, D), (D * TOKENS) ** -0.5, 0.0012207031)
    up_query = gaussian(key_of[8], (ADAPTER_RANK, HH), (HH * TOKENS) ** -0.5, 0.0014648438)
    down_value = gaussian(key_of[9], (ADAPTER_RANK, D), (D * TOKENS) ** -0.5, 0.0012207031)
    up_value = gaussian(key_of[10], (ADAPTER_RANK, HH), (HH * TOKENS) ** -0.5, 0.0014648438)
    return {"hidden": hidden, "queries": queries, "key_states": key_states, "value_states": value_states, "attention_out": attention_out, "grad_out": grad_out, "lengths": lengths, "down_query": down_query, "up_query": up_query, "down_value": down_value, "up_value": up_value}


def pack_begin(lengths_row, total):
    seq_ends = jnp.cumsum(lengths_row).astype(jnp.int32)
    starts = (seq_ends - lengths_row).astype(jnp.int32)
    positions = jnp.arange(total, dtype=jnp.int32)
    inside = (positions[:, None] >= starts[None, :]) & (positions[:, None] < seq_ends[None, :])
    return lax.optimization_barrier(jnp.sum(jnp.where(inside, starts[None, :], 0), axis=1)).astype(jnp.int32)

def rotate_back(grads, seq_positions):
    rows = grads.shape[0]
    half = HD // 2
    inverse = jnp.exp(-(jnp.arange(half, dtype=jnp.float32) * (2.0 / HD)) * math.log(10000.0))
    angles = seq_positions.astype(jnp.float32)[:, None] * inverse[None, :]
    cosine = jnp.cos(angles)[:, None, :]
    sine = jnp.sin(angles)[:, None, :]
    split = grads.astype(jnp.float32).reshape(rows, H, HD)
    first = split[:, :, :half]
    second = split[:, :, half:]
    new_first = first * cosine + second * sine
    new_second = second * cosine - first * sine
    joined = jnp.concatenate([new_first, new_second], axis=2)
    return joined.reshape(rows, H * HD).astype(jnp.bfloat16)

def head_grads(operands, begin):
    head_query, head_key, head_value, head_out, head_grad = operands
    total = head_query.shape[0]
    scaling = 1.0 / math.sqrt(HD)
    positions = jnp.arange(total, dtype=jnp.int32)
    allowed = (positions[None, :] >= begin[:, None]) & (positions[None, :] <= positions[:, None])
    scores = jnp.dot(head_query, head_key.T, preferred_element_type=jnp.float32) * scaling
    masked = jnp.where(allowed, scores, -1e+30)
    row_top = lax.optimization_barrier(jnp.max(masked, axis=1, keepdims=True))
    weights = jnp.where(allowed, jnp.exp(masked - row_top), 0.0)
    prob_rows = weights / lax.optimization_barrier(jnp.sum(weights, axis=1, keepdims=True))
    prob_low = prob_rows.astype(jnp.bfloat16)
    grad_prob = jnp.dot(head_grad, head_value.T, preferred_element_type=jnp.float32)
    row_delta = lax.optimization_barrier(jnp.sum(head_out.astype(jnp.float32) * head_grad.astype(jnp.float32), axis=1, keepdims=True))
    grad_score = (prob_rows * (grad_prob - row_delta)).astype(jnp.bfloat16)
    grad_query = (jnp.dot(grad_score, head_key, preferred_element_type=jnp.float32) * scaling).astype(jnp.bfloat16)
    grad_key = (jnp.dot(grad_score.T, head_query, preferred_element_type=jnp.float32) * scaling).astype(jnp.bfloat16)
    grad_value = jnp.dot(prob_low.T, head_grad, preferred_element_type=jnp.float32).astype(jnp.bfloat16)
    return (grad_query, grad_key, grad_value)

def pack_grads(operands):
    pack_query, pack_key, pack_value, pack_out, pack_grad, lengths_row = operands
    total = pack_query.shape[0]
    begin = pack_begin(lengths_row, total)

    def split_heads(array):
        return array.reshape(total, H, HD).transpose(1, 0, 2)

    def one_head(head_operands):
        return head_grads(head_operands, begin)
    split_inputs = (split_heads(pack_query), split_heads(pack_key), split_heads(pack_value), split_heads(pack_out), split_heads(pack_grad))
    grad_query, grad_key, grad_value = lax.map(one_head, split_inputs)

    def join_heads(array):
        return array.transpose(1, 0, 2).reshape(total, H * HD)
    seq_positions = (jnp.arange(total, dtype=jnp.int32) - begin).astype(jnp.int32)
    return (join_heads(grad_query), join_heads(grad_key), join_heads(grad_value), seq_positions)

def reference(hidden, queries, key_states, value_states, attention_out, grad_out, lengths, down_query, up_query, down_value, up_value):

    def packed(array):
        return array.reshape(N_DP, S, H * HD)
    grad_queries, grad_keys, value_gradients, seq_positions = lax.map(pack_grads, (packed(queries), packed(key_states), packed(value_states), packed(attention_out), packed(grad_out), lengths))
    grad_queries = grad_queries.reshape(TOKENS, H * HD)
    grad_keys = grad_keys.reshape(TOKENS, H * HD)
    value_gradients = value_gradients.reshape(TOKENS, H * HD)
    seq_positions = seq_positions.reshape(TOKENS)
    query_gradient_before = rotate_back(grad_queries, seq_positions)
    adapter_scale = ADAPTER_ALPHA / ADAPTER_RANK
    query_lowrank = jnp.dot(hidden, down_query.T, preferred_element_type=jnp.float32).astype(jnp.bfloat16)
    value_lowrank = jnp.dot(hidden, down_value.T, preferred_element_type=jnp.float32).astype(jnp.bfloat16)
    query_backprop = jnp.dot(query_gradient_before, up_query.T, preferred_element_type=jnp.float32).astype(jnp.bfloat16)
    value_backprop = jnp.dot(value_gradients, up_value.T, preferred_element_type=jnp.float32).astype(jnp.bfloat16)
    query_down_gradient = adapter_scale * jnp.dot(query_backprop.T, hidden, preferred_element_type=jnp.float32)
    query_up_gradient = adapter_scale * jnp.dot(query_lowrank.T, query_gradient_before, preferred_element_type=jnp.float32)
    value_down_gradient = adapter_scale * jnp.dot(value_backprop.T, hidden, preferred_element_type=jnp.float32)
    value_up_gradient = adapter_scale * jnp.dot(value_lowrank.T, value_gradients, preferred_element_type=jnp.float32)
    return (grad_queries, grad_keys, value_gradients, query_down_gradient, query_up_gradient, value_down_gradient, value_up_gradient)
```

```python
import functools
import math

import jax
import jax.numpy as jnp
from jax import lax
from jax.experimental import pallas as pl
from jax.experimental.pallas import tpu as pltpu
from jax.sharding import PartitionSpec as P

H = 32
HD = 128
RANK = 8
ADAPTER_ALPHA = 16
SCALING = 1.0 / math.sqrt(HD)
LOG2E = 1.4426950408889634
BF16 = jnp.bfloat16
F32 = jnp.float32
NT = (((1,), (1,)), ((), ()))
VMEM_LIMIT = 56 * 1024 * 1024


def params():
    return pltpu.CompilerParams(vmem_limit_bytes=VMEM_LIMIT)


def any_specs(count):
    return [pl.BlockSpec(memory_space=pl.ANY)] * count


def vmem_specs(count):
    return [pl.BlockSpec(memory_space=pltpu.VMEM)] * count


def dot_nt(left, right):
    return lax.dot_general(left, right, NT, preferred_element_type=F32)


def two_parts(value):
    high = value.astype(BF16)
    low = (value - high.astype(F32)).astype(BF16)
    return high, low


def three_parts(value):
    high, _ = two_parts(value)
    rest = value - high.astype(F32)
    middle, low = two_parts(rest)
    return high, middle, low


def pack_kernel(members, heads_here, first_head, stage_heads, *refs):
    sources = refs[:4]
    messages = refs[4 : 4 + members]
    sems = refs[4 + members]
    me = lax.axis_index("seq")
    copies = []
    for offset in range(members):
        target = me ^ offset
        start = pl.multiple_of((target * heads_here + first_head) * HD, HD)
        for which in range(4):
            copies.append(
                pltpu.make_async_copy(
                    sources[which].at[:, pl.ds(start, stage_heads * HD)],
                    messages[offset].at[which],
                    sems.at[offset, which],
                )
            )
    for copy in copies:
        copy.start()
    for copy in copies:
        copy.wait()


def pack(sources, members, heads_here, first_head, stage_heads):
    rows = sources[0].shape[0]
    shape = jax.ShapeDtypeStruct((4, rows, stage_heads * HD), BF16)
    size = 2 * 4 * rows * stage_heads * HD * members * 2
    return pl.pallas_call(
        functools.partial(pack_kernel, members, heads_here, first_head, stage_heads),
        out_shape=[shape] * members,
        in_specs=any_specs(4),
        out_specs=any_specs(members),
        scratch_shapes=[pltpu.SemaphoreType.DMA((members, 4))],
        compiler_params=params(),
        cost_estimate=pl.CostEstimate(flops=0, bytes_accessed=size, transcendentals=0),
        name="pack",
    )(*sources)


def side_kernel(members, heads_here, out_ref, grad_ref, hidden_ref, downq_ref, downv_ref, *refs):
    messages = refs[:members]
    held, sems = refs[members:]
    me = lax.axis_index("seq")
    low_query = dot_nt(downq_ref[...], hidden_ref[...]).astype(BF16)
    low_value = dot_nt(downv_ref[...], hidden_ref[...]).astype(BF16)
    rows = out_ref.shape[0]
    ones = jnp.ones((8, HD), BF16)
    for member in range(members):
        parts = []
        for head in range(heads_here):
            low_col = (member * heads_here + head) * HD
            product = out_ref[:, low_col : low_col + HD].astype(F32) * grad_ref[
                :, low_col : low_col + HD
            ].astype(F32)
            high, middle, low = three_parts(product)
            total = dot_nt(ones, high) + (dot_nt(ones, middle) + dot_nt(ones, low))
            parts.extend(three_parts(total[0:1, :]))
        parts.append(jnp.zeros((16 - 3 * heads_here, rows), BF16))
        held[member] = jnp.concatenate(parts + [low_query, low_value], axis=0)
    copies = [
        pltpu.make_async_copy(held.at[me ^ offset], messages[offset], sems.at[offset])
        for offset in range(members)
    ]
    for copy in copies:
        copy.start()
    for copy in copies:
        copy.wait()


def side(attention_out, grad_out, hidden, down_query, down_value, members, heads_here):
    rows = hidden.shape[0]
    return pl.pallas_call(
        functools.partial(side_kernel, members, heads_here),
        out_shape=[jax.ShapeDtypeStruct((32, rows), BF16)] * members,
        in_specs=vmem_specs(5),
        out_specs=any_specs(members),
        scratch_shapes=[
            pltpu.VMEM((members, 32, rows), BF16),
            pltpu.SemaphoreType.DMA((members,)),
        ],
        compiler_params=params(),
        cost_estimate=pl.CostEstimate(flops=10**9, bytes_accessed=4 * 2**20, transcendentals=0),
        name="side",
    )(attention_out, grad_out, hidden, down_query, down_value)


def begin_of(lengths_ref, positions):
    begin = jnp.zeros_like(positions)
    start = jnp.int32(0)
    for index in range(lengths_ref.shape[1] - 1):
        start = start + lengths_ref[0, index]
        begin = jnp.where(positions >= start, start, begin)
    return begin


def attention_kernel(
    members,
    heads_here,
    first_head,
    stage_heads,
    lengths_ref,
    upq_ref,
    upv_ref,
    cos_ref,
    sin_ref,
    *refs,
):
    refs = list(refs)
    messages = [refs.pop(0) for _ in range(members)]
    sides = [refs.pop(0) for _ in range(members)]
    outs = [refs.pop(0) for _ in range(members)]
    back_ref = refs.pop(0)
    terms_ref = refs.pop(0)
    held, side_held, key_flip, grads, key_acc, value_acc, in_sems, side_sems, out_sems = refs
    me = lax.axis_index("seq")
    rows = messages[0].shape[1]
    total = rows * members
    block = min(256, total)
    reach = total // 2
    rows_of = [
        pl.ds(pl.multiple_of((me ^ offset) * rows, rows), rows) for offset in range(members)
    ]
    copies = []
    for offset in range(members):
        copies.append(
            pltpu.make_async_copy(
                messages[offset], held.at[:, rows_of[offset], :], in_sems.at[offset]
            )
        )
        copies.append(
            pltpu.make_async_copy(
                sides[offset], side_held.at[:, rows_of[offset]], side_sems.at[offset]
            )
        )
    for copy in copies:
        copy.start()
    key_acc[...] = jnp.zeros_like(key_acc)
    value_acc[...] = jnp.zeros_like(value_acc)
    terms_ref[...] = jnp.zeros_like(terms_ref)
    for copy in copies:
        copy.wait()
    columns = [slice(head * HD, (head + 1) * HD) for head in range(stage_heads)]
    for head in range(stage_heads):
        key_flip[head] = held[1, :, columns[head]].astype(F32).T.astype(BF16)

    def query_block(low, key_low, width):
        positions = low + lax.broadcasted_iota(jnp.int32, (1, block), 1)
        begin = begin_of(lengths_ref, positions)
        key_positions = key_low + lax.broadcasted_iota(jnp.int32, (width, block), 0)
        allowed = (key_positions >= begin) & (key_positions <= positions)
        bias = jnp.where(allowed, 0.0, -1e30).astype(F32)
        here = pl.ds(low, block)
        keys_here = pl.ds(key_low, width)
        cosine = cos_ref[:, here]
        sine = sin_ref[:, here]
        back_query = jnp.zeros((RANK, block), F32)
        for head in range(stage_heads):
            cols = columns[head]
            query = held[0, here, cols]
            grad = held[3, here, cols]
            scores = dot_nt(held[1, keys_here, cols], query) + bias
            grad_prob = dot_nt(held[2, keys_here, cols], grad)
            top = jnp.max(scores, axis=0, keepdims=True)
            weights = jnp.exp2((scores - top) * (SCALING * LOG2E))
            inverse = 1.0 / jnp.sum(weights, axis=0, keepdims=True)
            probs = weights * inverse
            row = 3 * (first_head + head)
            parts = side_held[0:16, here].astype(F32)
            delta = parts[row : row + 1] + parts[row + 1 : row + 2] + parts[row + 2 : row + 3]
            grad_score = (probs * (grad_prob - delta)).astype(BF16)
            value_acc[head, keys_here, :] += jnp.dot(
                probs.astype(BF16), grad, preferred_element_type=F32
            )
            key_acc[head, keys_here, :] += jnp.dot(grad_score, query, preferred_element_type=F32)
            flipped = SCALING * jnp.dot(
                key_flip[head, :, keys_here], grad_score, preferred_element_type=F32
            )
            grads[0, here, cols] = flipped.T.astype(BF16)
            rounded = flipped.astype(BF16).astype(F32)
            first = rounded[: HD // 2]
            second = rounded[HD // 2 :]
            before = jnp.concatenate(
                [first * cosine + second * sine, second * cosine - first * sine], axis=0
            ).astype(BF16)
            back_query += jnp.dot(upq_ref[:, cols], before, preferred_element_type=F32)
            terms_ref[0:RANK, cols] += dot_nt(side_held[16:24, here], before)
        back_ref[0:RANK, here] = back_query

    if total <= 1024:
        for low in range(0, total, block):
            key_low = max(0, low - reach)
            query_block(low, key_low, low + block - key_low)
    else:

        @pl.loop(0, total // block)
        def _(index):
            low = pl.multiple_of(index * block, block)
            key_low = pl.multiple_of(jnp.maximum(low - reach, 0), block)
            query_block(low, key_low, reach + block)

    back_value = jnp.zeros((RANK, total), F32)
    for head in range(stage_heads):
        cols = columns[head]
        grads[1, :, cols] = (key_acc[head] * SCALING).astype(BF16)
        value_grad = value_acc[head].astype(BF16)
        grads[2, :, cols] = value_grad
        back_value += dot_nt(upv_ref[:, cols], value_grad)
        terms_ref[RANK : 2 * RANK, cols] = jnp.dot(
            side_held[24:32, :], value_grad, preferred_element_type=F32
        )
    back_ref[RANK : 2 * RANK, :] = back_value
    copies = [
        pltpu.make_async_copy(grads.at[:, rows_of[offset], :], outs[offset], out_sems.at[offset])
        for offset in range(members)
    ]
    for copy in copies:
        copy.start()
    for copy in copies:
        copy.wait()


def attention(lengths, ups, turns, messages, sides, heads_here, first_head, stage_heads):
    members = len(messages)
    rows = messages[0].shape[1]
    total = rows * members
    width = stage_heads * HD
    message = jax.ShapeDtypeStruct((3, rows, width), BF16)
    return pl.pallas_call(
        functools.partial(attention_kernel, members, heads_here, first_head, stage_heads),
        out_shape=[message] * members
        + [
            jax.ShapeDtypeStruct((2 * RANK, total), F32),
            jax.ShapeDtypeStruct((2 * RANK, width), F32),
        ],
        in_specs=[pl.BlockSpec(memory_space=pltpu.SMEM)] + vmem_specs(4) + any_specs(2 * members),
        out_specs=any_specs(members) + vmem_specs(2),
        scratch_shapes=[
            pltpu.VMEM((4, total, width), BF16),
            pltpu.VMEM((32, total), BF16),
            pltpu.VMEM((stage_heads, HD, total), BF16),
            pltpu.VMEM((3, total, width), BF16),
            pltpu.VMEM((stage_heads, total, HD), F32),
            pltpu.VMEM((stage_heads, total, HD), F32),
            pltpu.SemaphoreType.DMA((members,)),
            pltpu.SemaphoreType.DMA((members,)),
            pltpu.SemaphoreType.DMA((members,)),
        ],
        compiler_params=params(),
        cost_estimate=pl.CostEstimate(
            flops=stage_heads * 5 * 10**9, bytes_accessed=4 * 2**20, transcendentals=0
        ),
        name="attention",
    )(lengths, *ups, *turns, *messages, *sides)


def spread_kernel(members, stages, *refs):
    backs = refs[:stages]
    messages = refs[stages : stages + members]
    held, sems = refs[stages + members :]
    me = lax.axis_index("seq")
    rows = held.shape[2]
    for member in range(members):
        here = slice(member * rows, (member + 1) * rows)
        total = backs[0][:, here]
        for back in backs[1:]:
            total = total + back[:, here]
        high, low = two_parts(total)
        held[member] = jnp.concatenate([high, low], axis=0)
    copies = [
        pltpu.make_async_copy(held.at[me ^ offset], messages[offset], sems.at[offset])
        for offset in range(members)
    ]
    for copy in copies:
        copy.start()
    for copy in copies:
        copy.wait()


def spread(backs, members, rows):
    return pl.pallas_call(
        functools.partial(spread_kernel, members, len(backs)),
        out_shape=[jax.ShapeDtypeStruct((4 * RANK, rows), BF16)] * members,
        in_specs=vmem_specs(len(backs)),
        out_specs=any_specs(members),
        scratch_shapes=[
            pltpu.VMEM((members, 4 * RANK, rows), BF16),
            pltpu.SemaphoreType.DMA((members,)),
        ],
        compiler_params=params(),
        cost_estimate=pl.CostEstimate(flops=10**6, bytes_accessed=10**5, transcendentals=0),
        name="spread",
    )(*backs)


def down_kernel(members, packs, stage_sizes, hidden_ref, *refs):
    backs = refs[:members]
    ups = refs[members : members + len(stage_sizes)]
    messages = refs[members + len(stage_sizes) : members + len(stage_sizes) + packs]
    held, sems = refs[members + len(stage_sizes) + packs :]
    me = lax.axis_index("seq")
    pack_here = lax.axis_index("dp")
    total = backs[0][...].astype(F32)
    for back in backs[1:]:
        total = total + back[...].astype(F32)
    back = (total[: 2 * RANK] + total[2 * RANK :]).astype(BF16)
    terms = jnp.dot(back, hidden_ref[...], preferred_element_type=F32)
    down_cols = terms.shape[1] // packs
    sharers = members // packs
    head_cols = sum(stage_sizes) * HD
    for target in range(packs):
        held[target, :, :down_cols] = terms[:, target * down_cols : (target + 1) * down_cols]
        for place in range(sharers):
            low = down_cols + place * head_cols
            mine = me == target * sharers + place
            for size, up in zip(stage_sizes, ups):
                held[target, :, low : low + size * HD] = jnp.where(mine, up[...], 0.0)
                low += size * HD
    copies = [
        pltpu.make_async_copy(held.at[pack_here ^ offset], messages[offset], sems.at[offset])
        for offset in range(packs)
    ]
    for copy in copies:
        copy.start()
    for copy in copies:
        copy.wait()


def down_terms(hidden, backs, ups, packs):
    members = len(backs)
    stage_sizes = [up.shape[1] // HD for up in ups]
    width = hidden.shape[1] // packs + (members // packs) * sum(stage_sizes) * HD
    return pl.pallas_call(
        functools.partial(down_kernel, members, packs, stage_sizes),
        out_shape=[jax.ShapeDtypeStruct((2 * RANK, width), F32)] * packs,
        in_specs=vmem_specs(1 + members + len(ups)),
        out_specs=any_specs(packs),
        scratch_shapes=[
            pltpu.VMEM((packs, 2 * RANK, width), F32),
            pltpu.SemaphoreType.DMA((packs,)),
        ],
        compiler_params=params(),
        cost_estimate=pl.CostEstimate(flops=10**7, bytes_accessed=2 * 10**6, transcendentals=0),
        name="down_terms",
    )(hidden, *backs, *ups)


def unpack_kernel(members, heads_here, stages, *refs):
    count = members * len(stages)
    messages = refs[:count]
    outs = refs[count : count + 3]
    sems = refs[count + 3]
    me = lax.axis_index("seq")
    copies = []
    for stage, (first_head, stage_heads) in enumerate(stages):
        for offset in range(members):
            source = me ^ offset
            start = pl.multiple_of((source * heads_here + first_head) * HD, HD)
            for which in range(3):
                copies.append(
                    pltpu.make_async_copy(
                        messages[stage * members + offset].at[which],
                        outs[which].at[:, pl.ds(start, stage_heads * HD)],
                        sems.at[stage, offset, which],
                    )
                )
    for copy in copies:
        copy.start()
    for copy in copies:
        copy.wait()


def unpack(messages, members, heads_here, stages):
    rows = messages[0].shape[1]
    width = members * heads_here * HD
    return pl.pallas_call(
        functools.partial(unpack_kernel, members, heads_here, stages),
        out_shape=[jax.ShapeDtypeStruct((rows, width), BF16)] * 3,
        in_specs=any_specs(len(messages)),
        out_specs=any_specs(3),
        scratch_shapes=[pltpu.SemaphoreType.DMA((len(stages), members, 3))],
        compiler_params=params(),
        cost_estimate=pl.CostEstimate(
            flops=0, bytes_accessed=2 * 3 * rows * width * 2, transcendentals=0
        ),
        name="unpack",
    )(*messages)


def exchange(messages, axis):
    count = len(messages)
    return [messages[0]] + [
        lax.ppermute(messages[offset], axis, [(i, i ^ offset) for i in range(count)])
        for offset in range(1, count)
    ]


def turn_tables(lengths_row, total):
    positions = jnp.arange(total, dtype=jnp.int32)
    ends = jnp.cumsum(lengths_row)
    starts = ends - lengths_row
    begin = jnp.max(jnp.where(positions[:, None] >= starts[None, :], starts[None, :], 0), axis=1)
    half = HD // 2
    inverse = jnp.exp(-(jnp.arange(half, dtype=F32) * (2.0 / HD)) * math.log(10000.0))
    angles = inverse[:, None] * (positions - begin).astype(F32)[None, :]
    return jnp.cos(angles), jnp.sin(angles)


def shards(
    hidden,
    queries,
    key_states,
    value_states,
    attention_out,
    grad_out,
    lengths,
    down_query,
    up_query,
    down_value,
    up_value,
):
    rows = queries.shape[0]
    members = lax.axis_size("seq")
    packs = lax.axis_size("dp")
    total = rows * members
    heads_here = H // members
    stages = [(0, heads_here)]
    if heads_here > 1:
        stages = [(0, heads_here // 2), (heads_here // 2, heads_here - heads_here // 2)]
    sources = (queries, key_states, value_states, grad_out)
    me = lax.axis_index("seq")

    arrived = []
    sides = None
    for first_head, stage_heads in stages:
        packed = pack(sources, members, heads_here, first_head, stage_heads)
        arrived.append(exchange(packed, "seq"))
        if sides is None:
            sides = exchange(
                side(
                    attention_out, grad_out, hidden, down_query, down_value, members, heads_here
                ),
                "seq",
            )
    turns = turn_tables(lengths[0], total)
    returned = []
    backs = []
    ups = []
    for (first_head, stage_heads), messages in zip(stages, arrived):
        start = (me * heads_here + first_head) * HD
        up_here = tuple(
            lax.dynamic_slice_in_dim(up, start, stage_heads * HD, 1) for up in (up_query, up_value)
        )
        *grads, back, up_terms = attention(
            lengths, up_here, turns, messages, sides, heads_here, first_head, stage_heads
        )
        returned.append(grads)
        backs.append(back)
        ups.append(up_terms)
    back_messages = exchange(spread(backs, members, rows), "seq")
    home = []
    for grads in returned:
        home.extend(exchange(grads, "seq"))
    pieces = exchange(down_terms(hidden, back_messages, ups, packs), "dp")
    summed = pieces[0]
    for piece in pieces[1:]:
        summed = summed + piece
    step = 1
    while step < members:
        summed = summed + lax.ppermute(summed, "seq", [(i, i ^ step) for i in range(members)])
        step *= 2
    summed = summed * (ADAPTER_ALPHA / RANK)
    down_cols = hidden.shape[1] // packs
    grad_queries, grad_keys, value_gradients = unpack(home, members, heads_here, stages)
    return (
        grad_queries,
        grad_keys,
        value_gradients,
        summed[:RANK, :down_cols],
        summed[:RANK, down_cols:],
        summed[RANK:, :down_cols],
        summed[RANK:, down_cols:],
    )


def solution(mesh):
    tokens = P(("dp", "seq"), None)
    placed = (tokens,) * 6 + (P("dp", None),) + (P(),) * 4
    return jax.shard_map(
        shards,
        mesh=mesh,
        in_specs=placed,
        out_specs=(tokens,) * 3 + (P(None, "dp"),) * 4,
        check_vma=False,
    )
```

```python
import functools
import math

import jax
import jax.numpy as jnp
from jax import lax
from jax.experimental import pallas as pl
from jax.experimental.pallas import tpu as pltpu
from jax.sharding import PartitionSpec as P

H = 32
HD = 128
RANK = 8
ADAPTER_ALPHA = 16
SCALING = 1.0 / math.sqrt(HD)
LOG2E = 1.4426950408889634
BF16 = jnp.bfloat16
F32 = jnp.float32
NT = (((1,), (1,)), ((), ()))
MIB = 1024 * 1024
COST = pl.CostEstimate(flops=0, bytes_accessed=0, transcendentals=0)
ATTENTION_COST = pl.CostEstimate(flops=10**10, bytes_accessed=0, transcendentals=0)
WHOLE_IN = (False, False)
WHOLE_OUT = (False, False)
ORDER = (6, 2, 4, 7, 3, 5, 1)
CHAIN = tuple((place, max(1, place - 3)) for place in range(1, 8))
PLAN = (
    ((6, 2, 4), ()),
    ((), ()),
    ((7, 3), ()),
    ((5, 1), (6, 2)),
    ((), (4,)),
)


def params(mebibytes):
    return pltpu.CompilerParams(vmem_limit_bytes=mebibytes * MIB)


def offsets_of(count):
    return (0,) + ORDER if count == 1 + len(ORDER) else tuple(range(count))


def pair_offsets(members):
    return [offset for offset in offsets_of(members) if offset % 2 == 0]


def part_of(refs, me, offset):
    if len(refs) == 1:
        return refs[0].at[me ^ offset]
    return refs[offsets_of(len(refs)).index(offset)]


def group_shapes(whole, members, shape, dtype):
    if whole:
        return [jax.ShapeDtypeStruct((members,) + shape, dtype)]
    return [jax.ShapeDtypeStruct(shape, dtype)] * members


def any_specs(count):
    return [pl.BlockSpec(memory_space=pl.ANY)] * count


def vmem_specs(count):
    return [pl.BlockSpec(memory_space=pltpu.VMEM)] * count


def dot_nt(left, right):
    return lax.dot_general(left, right, NT, preferred_element_type=F32)


def two_parts(value):
    high = value.astype(BF16)
    low = (value - high.astype(F32)).astype(BF16)
    return high, low


def three_parts(value):
    high, _ = two_parts(value)
    rest = value - high.astype(F32)
    middle, low = two_parts(rest)
    return high, middle, low


def side_rows(out_ref, grad_ref, hidden_ref, downq_ref, downv_ref):
    product = out_ref[...].astype(F32) * grad_ref[...].astype(F32)
    heads_at = lax.broadcasted_iota(jnp.int32, (H * HD, 128), 0) // HD
    lanes = lax.broadcasted_iota(jnp.int32, (H * HD, 128), 1)
    pick = jnp.where(heads_at == lanes, 1.0, 0.0).astype(BF16)
    high, middle, low = (
        jnp.dot(part, pick, preferred_element_type=F32) for part in three_parts(product)
    )
    delta = (high + (middle + low)).T[:H]
    downs = jnp.concatenate([downq_ref[...], downv_ref[...]], axis=0)
    return three_parts(delta), dot_nt(downs, hidden_ref[...]).astype(BF16)


def pack_kernel(members, heads_here, first_head, stage_heads, with_side, whole, *refs):
    refs = list(refs)
    sources = [refs.pop(0) for _ in range(4)]
    side_refs = [refs.pop(0) for _ in range(5 if with_side else 0)]
    messages = [refs.pop(0) for _ in range(1 if whole else members)]
    held, in_sems, out_sems = refs
    me = lax.axis_index("seq")
    rows = sources[0].shape[0]
    reads = []
    for offset in range(members):
        target = me ^ offset
        for head in range(stage_heads):
            start = pl.multiple_of((target * heads_here + first_head + head) * HD, HD)
            for which in range(4):
                place = head * 4 + which
                reads.append(
                    pltpu.make_async_copy(
                        sources[which].at[:, pl.ds(start, HD)],
                        held.at[target, place * rows : (place + 1) * rows],
                        in_sems.at[offset, place],
                    )
                )
    writes = [
        pltpu.make_async_copy(
            held.at[me ^ offset], part_of(messages, me, offset), out_sems.at[offset]
        )
        for offset in range(members)
    ]
    for copy in reads:
        copy.start()
    if with_side:
        parts, lows = side_rows(*side_refs)
        blank = jnp.zeros((16 - 3 * heads_here, rows), BF16)
        for member in range(members):
            here = slice(member * heads_here, (member + 1) * heads_here)
            held[member, 4 * stage_heads * rows :] = jnp.concatenate(
                [part[here] for part in parts] + [blank, lows], axis=0
            )
    per_message = 4 * stage_heads
    for offset in range(members):
        for place in range(per_message):
            reads[offset * per_message + place].wait()
        writes[offset].start()
    for copy in writes:
        copy.wait()


def pack(sources, side_sources, members, heads_here, first_head, stage_heads, whole):
    rows = sources[0].shape[0]
    shape = (4 * stage_heads * rows + (32 if side_sources else 0), HD)
    size = 2 * 4 * rows * stage_heads * HD * members * 2
    return pl.pallas_call(
        functools.partial(
            pack_kernel, members, heads_here, first_head, stage_heads, bool(side_sources), whole
        ),
        out_shape=group_shapes(whole, members, shape, BF16),
        in_specs=any_specs(4) + vmem_specs(len(side_sources)),
        out_specs=any_specs(1 if whole else members),
        scratch_shapes=[
            pltpu.VMEM((members,) + shape, BF16),
            pltpu.SemaphoreType.DMA((members, 4 * stage_heads)),
            pltpu.SemaphoreType.DMA((members,)),
        ],
        compiler_params=params(56),
        cost_estimate=COST,
        name="pack",
    )(*sources, *side_sources)


def begin_of(lengths_ref, positions):
    begin = jnp.int32(0) * positions
    start = jnp.int32(0)
    for index in range(lengths_ref.shape[1] - 1):
        start = start + lengths_ref[0, index]
        begin = jnp.where(positions >= start, start, begin)
    return begin


def attention_kernel(
    members,
    heads_here,
    first_head,
    stage_heads,
    counts,
    lengths_ref,
    upq_ref,
    upv_ref,
    cos_ref,
    sin_ref,
    *refs,
):
    refs = list(refs)
    messages, sides, outs, backs = [], [], [], []
    for group, count in zip((messages, sides), counts):
        group.extend(refs.pop(0) for _ in range(count))
    sides = sides or messages
    earlier_back = None if first_head == 0 else refs.pop(0)
    for group, count in zip((outs, backs), counts[2:]):
        group.extend(refs.pop(0) for _ in range(count))
    last = first_head + stage_heads == heads_here
    terms_ref = refs.pop(0)
    held, side_held, key_flip, grads, key_acc, value_acc, back_ref = refs[:7]
    in_sems, side_sems, out_sems = refs[7:]
    me = lax.axis_index("seq")
    total = held.shape[1]
    rows = total // members
    side_low = sides[0].shape[-2] - 32
    block = min(256, total)
    reach = total // 2
    rows_of = [
        pl.ds(pl.multiple_of((me ^ offset) * rows, rows), rows) for offset in range(members)
    ]
    copies = []
    for offset in range(members):
        for place in range(4 * stage_heads):
            copies.append(
                pltpu.make_async_copy(
                    part_of(messages, me, offset).at[place * rows : (place + 1) * rows],
                    held.at[place, rows_of[offset], :],
                    in_sems.at[offset, place],
                )
            )
        copies.append(
            pltpu.make_async_copy(
                part_of(sides, me, offset).at[side_low : side_low + 32],
                side_held.at[:, rows_of[offset]],
                side_sems.at[offset],
            )
        )
    for copy in copies:
        copy.start()
    key_acc[...] = jnp.zeros_like(key_acc)
    value_acc[...] = jnp.zeros_like(value_acc)
    terms_ref[...] = jnp.zeros_like(terms_ref)
    for copy in copies:
        copy.wait()
    columns = [slice(head * HD, (head + 1) * HD) for head in range(stage_heads)]
    for head in range(stage_heads):
        key_flip[head] = held[4 * head + 1].astype(F32).T.astype(BF16)

    def query_block(low, key_low, width):
        positions = low + lax.broadcasted_iota(jnp.int32, (1, block), 1)
        begin = begin_of(lengths_ref, positions)
        key_positions = key_low + lax.broadcasted_iota(jnp.int32, (width, block), 0)
        allowed = (key_positions >= begin) & (key_positions <= positions)
        bias = jnp.where(allowed, 0.0, -1e30).astype(F32)
        here = pl.ds(low, block)
        keys_here = pl.ds(key_low, width)
        cosine = cos_ref[:, here]
        sine = sin_ref[:, here]
        back_query = jnp.zeros((RANK, block), F32)
        parts = side_held[0:16, here].astype(F32)
        for head in range(stage_heads):
            cols = columns[head]
            query = held[4 * head, here, :]
            grad = held[4 * head + 3, here, :]
            scores = dot_nt(held[4 * head + 1, keys_here, :], query) + bias
            grad_prob = dot_nt(held[4 * head + 2, keys_here, :], grad)
            top = jnp.max(scores, axis=0, keepdims=True)
            weights = jnp.exp2((scores - top) * (SCALING * LOG2E))
            inverse = 1.0 / jnp.sum(weights, axis=0, keepdims=True)
            probs = weights * inverse
            row = first_head + head
            delta = sum(
                parts[place : place + 1] for place in range(row, 3 * heads_here, heads_here)
            )
            grad_score = (probs * (grad_prob - delta)).astype(BF16)
            value_acc[head, keys_here, :] += jnp.dot(
                probs.astype(BF16), grad, preferred_element_type=F32
            )
            key_acc[head, keys_here, :] += jnp.dot(grad_score, query, preferred_element_type=F32)
            flipped = SCALING * jnp.dot(
                key_flip[head, :, keys_here], grad_score, preferred_element_type=F32
            )
            grads[0, here, cols] = flipped.T.astype(BF16)
            rounded = flipped.astype(BF16).astype(F32)
            first = rounded[: HD // 2]
            second = rounded[HD // 2 :]
            before = jnp.concatenate(
                [first * cosine + second * sine, second * cosine - first * sine], axis=0
            ).astype(BF16)
            back_query += jnp.dot(upq_ref[:, cols], before, preferred_element_type=F32)
            terms_ref[0:RANK, cols] += dot_nt(side_held[16:24, here], before)
        back_ref[0:RANK, here] = back_query

    widths = [block + part * reach // 4 for part in range(5)]

    @pl.loop(0, total // block)
    def _(index):
        low = pl.multiple_of(index * block, block)
        needed = low + block - begin_of(lengths_ref, low)
        for place, width in enumerate(widths):
            fits = needed <= width
            if place:
                fits = fits & (needed > widths[place - 1])

            @pl.when(fits)
            def _(width=width):
                key_low = pl.multiple_of(jnp.maximum(low + block - width, 0), 128)
                query_block(low, key_low, width)

    back_value = jnp.zeros((RANK, total), F32)
    for head in range(stage_heads):
        cols = columns[head]
        grads[1, :, cols] = (key_acc[head] * SCALING).astype(BF16)
        value_grad = value_acc[head].astype(BF16)
        grads[2, :, cols] = value_grad
        back_value += dot_nt(upv_ref[:, cols], value_grad)
        terms_ref[RANK : 2 * RANK, cols] = jnp.dot(
            side_held[24:32, :], value_grad, preferred_element_type=F32
        )
    back_ref[RANK : 2 * RANK, :] = back_value
    copies = [
        pltpu.make_async_copy(
            grads.at[:, rows_of[offset], :], part_of(outs, me, offset), out_sems.at[offset]
        )
        for offset in range(members)
    ]
    for copy in copies:
        copy.start()
    back = back_ref[...]
    if earlier_back is not None:
        back = back + earlier_back[...]
    if last:
        back_ref[...] = back
        for place, offset in enumerate(pair_offsets(members)):
            for group, flip in zip(backs, (0, 1)):
                group[place] = back_ref[:, rows_of[offset ^ flip]]
    else:
        backs[0][...] = back
    for copy in copies:
        copy.wait()


def attention(
    lengths,
    ups,
    turns,
    messages,
    sides,
    earlier_back,
    heads_here,
    first_head,
    stage_heads,
    members,
    rows,
    whole_out,
):
    total = rows * members
    width = stage_heads * HD
    last = first_head + stage_heads == heads_here
    out_shapes = group_shapes(whole_out, members, (3, rows, width), BF16)
    back_shapes = [jax.ShapeDtypeStruct((2 * RANK, total), F32)]
    if last:
        back_shapes = [jax.ShapeDtypeStruct((members // 2, 2 * RANK, rows), F32)] * 2
    earlier = [] if first_head == 0 else list(sides) + [earlier_back]
    counts = (len(messages), len(earlier[:-1]), len(out_shapes), len(back_shapes))
    results = pl.pallas_call(
        functools.partial(attention_kernel, members, heads_here, first_head, stage_heads, counts),
        out_shape=out_shapes + back_shapes + [jax.ShapeDtypeStruct((2 * RANK, width), F32)],
        in_specs=[pl.BlockSpec(memory_space=pltpu.SMEM)]
        + vmem_specs(4)
        + any_specs(len(messages))
        + (any_specs(len(sides)) + vmem_specs(1) if earlier else []),
        out_specs=any_specs(len(out_shapes)) + vmem_specs(len(back_shapes) + 1),
        scratch_shapes=[
            pltpu.VMEM((4 * stage_heads, total, HD), BF16),
            pltpu.VMEM((32, total), BF16),
            pltpu.VMEM((stage_heads, HD, total), BF16),
            pltpu.VMEM((3, total, width), BF16),
            pltpu.VMEM((stage_heads, total, HD), F32),
            pltpu.VMEM((stage_heads, total, HD), F32),
            pltpu.VMEM((2 * RANK, total), F32),
            pltpu.SemaphoreType.DMA((members, 4 * stage_heads)),
            pltpu.SemaphoreType.DMA((members,)),
            pltpu.SemaphoreType.DMA((members,)),
        ],
        compiler_params=params(56),
        cost_estimate=ATTENTION_COST,
        name="attention",
    )(lengths, *ups, *turns, *messages, *earlier)
    split = len(out_shapes)
    return results[:split], results[split:-1], results[-1]


def fold_kernel(own_ref, other_ref, *outs):
    for place, out in enumerate(outs):
        out[...] = own_ref[place] + other_ref[place]


def fold(own, other):
    count = own.shape[0]
    return pl.pallas_call(
        fold_kernel,
        out_shape=[jax.ShapeDtypeStruct(own.shape[1:], F32)] * count,
        in_specs=vmem_specs(2),
        out_specs=vmem_specs(count),
        compiler_params=params(4),
        cost_estimate=COST,
        name="fold",
    )(own, other)


def down_kernel(members, packs, stage_sizes, hidden_ref, *refs):
    backs = refs[: members // 2]
    ups = refs[members // 2 : members // 2 + len(stage_sizes)]
    messages = refs[members // 2 + len(stage_sizes) :][:packs]
    held, sems = refs[members // 2 + len(stage_sizes) + packs :]
    me = lax.axis_index("seq")
    pack_here = lax.axis_index("dp")
    total = backs[0][...]
    for back in backs[1:]:
        total = total + back[...]
    terms = jnp.dot(total.astype(BF16), hidden_ref[...], preferred_element_type=F32)
    down_cols = terms.shape[1] // packs
    sharers = members // packs
    for target in range(packs):
        held[target, :, :down_cols] = terms[:, target * down_cols : (target + 1) * down_cols]
        low = down_cols
        for size, up in zip(stage_sizes, ups):
            held[target, :, low : low + size * HD] = jnp.where(
                me // sharers == target, up[...], 0.0
            )
            low += size * HD
    copies = [
        pltpu.make_async_copy(held.at[pack_here ^ offset], messages[offset], sems.at[offset])
        for offset in range(packs)
    ]
    for copy in copies:
        copy.start()
    for copy in copies:
        copy.wait()


def down_terms(hidden, backs, ups, members, packs):
    stage_sizes = [up.shape[1] // HD for up in ups]
    width = hidden.shape[1] // packs + sum(stage_sizes) * HD
    return pl.pallas_call(
        functools.partial(down_kernel, members, packs, stage_sizes),
        out_shape=[jax.ShapeDtypeStruct((2 * RANK, width), F32)] * packs,
        in_specs=vmem_specs(1 + len(backs) + len(ups)),
        out_specs=any_specs(packs),
        scratch_shapes=[
            pltpu.VMEM((packs, 2 * RANK, width), F32),
            pltpu.SemaphoreType.DMA((packs,)),
        ],
        compiler_params=params(8),
        cost_estimate=COST,
        name="down_terms",
    )(hidden, *backs, *ups)


def packs_kernel(sharers, down_cols, *refs):
    pieces, out = refs[:-1], refs[-1]
    me = lax.axis_index("seq")
    total = pieces[0][...]
    for piece in pieces[1:]:
        total = total + piece[...]
    out[:, :down_cols] = total[:, :down_cols]
    size = total.shape[1] - down_cols
    for place in range(sharers):
        low = down_cols + place * size
        out[:, low : low + size] = jnp.where(me % sharers == place, total[:, down_cols:], 0.0)


def sum_packs(pieces, sharers, down_cols):
    width = down_cols + sharers * (pieces[0].shape[1] - down_cols)
    return pl.pallas_call(
        functools.partial(packs_kernel, sharers, down_cols),
        out_shape=jax.ShapeDtypeStruct((2 * RANK, width), F32),
        in_specs=vmem_specs(len(pieces)),
        out_specs=vmem_specs(1)[0],
        compiler_params=params(4),
        cost_estimate=COST,
        name="sum_packs",
    )(*pieces)


def finish_kernel(down_cols, *refs):
    pieces, outs = refs[:-4], refs[-4:]
    total = pieces[0][...]
    for piece in pieces[1:]:
        total = total + piece[...]
    total = total * (ADAPTER_ALPHA / RANK)
    outs[0][...] = total[:RANK, :down_cols]
    outs[1][...] = total[:RANK, down_cols:]
    outs[2][...] = total[RANK:, :down_cols]
    outs[3][...] = total[RANK:, down_cols:]


def finish(pieces, down_cols):
    up_cols = pieces[0].shape[1] - down_cols
    return pl.pallas_call(
        functools.partial(finish_kernel, down_cols),
        out_shape=[jax.ShapeDtypeStruct((RANK, cols), F32) for cols in (down_cols, up_cols)] * 2,
        in_specs=vmem_specs(len(pieces)),
        out_specs=vmem_specs(4),
        compiler_params=params(4),
        cost_estimate=COST,
        name="finish",
    )(*pieces)


def unpack_kernel(members, heads_here, stages, counts, *refs):
    count = sum(counts)
    groups = [refs[sum(counts[:i]) : sum(counts[: i + 1])] for i in range(len(counts))]
    outs = refs[count : count + 3]
    held = refs[count + 3 : count + 3 + len(stages)]
    in_sems, out_sems = refs[count + 3 + len(stages) :]
    me = lax.axis_index("seq")
    reads = []
    writes = []
    for stage, (first_head, stage_heads) in enumerate(stages):
        for offset in range(members):
            source = me ^ offset
            start = pl.multiple_of((source * heads_here + first_head) * HD, HD)
            reads.append(
                pltpu.make_async_copy(
                    part_of(groups[stage], me, offset),
                    held[stage].at[offset],
                    in_sems.at[stage, offset],
                )
            )
            writes.append(
                [
                    pltpu.make_async_copy(
                        held[stage].at[offset, which],
                        outs[which].at[:, pl.ds(start, stage_heads * HD)],
                        out_sems.at[stage, offset, which],
                    )
                    for which in range(3)
                ]
            )
    for copy in reads:
        copy.start()
    for copy, followers in zip(reads, writes):
        copy.wait()
        for follower in followers:
            follower.start()
    for followers in writes:
        for follower in followers:
            follower.wait()


def unpack(groups, members, heads_here, stages):
    rows = groups[0][0].shape[-2]
    counts = [len(group) for group in groups]
    messages = [message for group in groups for message in group]
    width = members * heads_here * HD
    return pl.pallas_call(
        functools.partial(unpack_kernel, members, heads_here, stages, counts),
        out_shape=[jax.ShapeDtypeStruct((rows, width), BF16)] * 3,
        in_specs=any_specs(len(messages)),
        out_specs=any_specs(3),
        scratch_shapes=[
            pltpu.VMEM((members, 3, rows, stage_heads * HD), BF16) for _, stage_heads in stages
        ]
        + [
            pltpu.SemaphoreType.DMA((len(stages), members)),
            pltpu.SemaphoreType.DMA((len(stages), members, 3)),
        ],
        compiler_params=params(56),
        cost_estimate=COST,
        name="unpack",
    )(*messages)


def exchange(messages, axis):
    count = len(messages)
    if count == 1:
        return [lax.all_to_all(messages[0], axis, split_axis=0, concat_axis=0, tiled=True)]
    return [
        lax.ppermute(message, axis, [(i, i ^ offset) for i in range(count)]) if offset else message
        for offset, message in zip(offsets_of(count), messages)
    ]


def turn_tables(lengths_row, total):
    positions = jnp.arange(total, dtype=jnp.int32)
    ends = jnp.cumsum(lengths_row)
    starts = ends - lengths_row
    begin = jnp.max(jnp.where(positions[:, None] >= starts[None, :], starts[None, :], 0), axis=1)
    half = HD // 2
    inverse = jnp.exp(-(jnp.arange(half, dtype=F32) * (2.0 / HD)) * math.log(10000.0))
    angles = inverse[:, None] * (positions - begin).astype(F32)[None, :]
    return jnp.cos(angles), jnp.sin(angles)


def shards(
    hidden,
    queries,
    key_states,
    value_states,
    attention_out,
    grad_out,
    lengths,
    down_query,
    up_query,
    down_value,
    up_value,
):
    rows = queries.shape[0]
    members = lax.axis_size("seq")
    packs = lax.axis_size("dp")
    total = rows * members
    heads_here = H // members
    stages = [(0, heads_here)]
    if heads_here > 1:
        stages = [(0, heads_here // 2), (heads_here // 2, heads_here - heads_here // 2)]
    sources = (queries, key_states, value_states, grad_out)
    me = lax.axis_index("seq")

    side_sources = (attention_out, grad_out, hidden, down_query, down_value)
    turns = turn_tables(lengths[0], total)
    packed = []
    for (first_head, stage_heads), whole in zip(stages, WHOLE_IN):
        extra = () if packed else side_sources
        held_back = sources
        if packed:
            held_back, _ = lax.optimization_barrier((sources, packed[0][0]))
        packed.append(
            list(pack(held_back, extra, members, heads_here, first_head, stage_heads, whole))
        )
    arrived = []
    home = []
    ups = []
    back = [None]
    planned = len(stages) == 2 and members == 8

    def after(value, stage, offsets):
        if not planned or not offsets:
            return value
        places = [offsets_of(members).index(offset) for offset in offsets]
        taken = tuple(home[stage][place] for place in places)
        value, taken = lax.optimization_barrier((value, taken))
        for place, message in zip(places, taken):
            home[stage][place] = message
        return value

    for index, (first_head, stage_heads) in enumerate(stages):
        arrived.append(exchange(packed[index], "seq"))
        if planned and index == 0:
            for place, before in CHAIN:
                packed[1][place], arrived[0][before] = lax.optimization_barrier(
                    (packed[1][place], arrived[0][before])
                )
        start = (me * heads_here + first_head) * HD
        up_here = tuple(
            lax.dynamic_slice_in_dim(up, start, stage_heads * HD, 1) for up in (up_query, up_value)
        )
        grads, back, up_terms = attention(
            lengths,
            up_here,
            turns,
            arrived[index],
            arrived[0],
            back[0],
            heads_here,
            first_head,
            stage_heads,
            members,
            rows,
            WHOLE_OUT[index],
        )
        home.append(exchange(grads, "seq"))
        ups.append(up_terms)
    def swap(value, offset):
        return lax.ppermute(value, "seq", [(i, i ^ offset) for i in range(members)])

    def planned_after(value, place):
        return after(after(value, 0, PLAN[place][0]), 1, PLAN[place][1])

    own, other = planned_after(tuple(back), 0)
    folded = planned_after(tuple(fold(own, swap(other, 1))), 1)
    tiles = [
        swap(tile, offset) if offset else tile
        for offset, tile in zip(pair_offsets(members), folded)
    ]
    tiles = planned_after(tiles, 2)
    pieces = exchange(down_terms(hidden, tiles, ups, members, packs), "dp")
    down_cols = hidden.shape[1] // packs
    summed = planned_after(sum_packs(pieces, members // packs, down_cols), 3)
    summed = planned_after(summed + swap(summed, 1), 4)
    if members == 8:
        pieces = [swap(summed, offset) if offset else summed for offset in pair_offsets(members)]
    else:
        step = 2
        while step < members // 2:
            summed = summed + swap(summed, step)
            step *= 2
        pieces = [summed, swap(summed, step)]
    down_query_grad, up_query_grad, down_value_grad, up_value_grad = finish(pieces, down_cols)
    grad_queries, grad_keys, value_gradients = unpack(home, members, heads_here, stages)
    return (
        grad_queries,
        grad_keys,
        value_gradients,
        down_query_grad,
        up_query_grad,
        down_value_grad,
        up_value_grad,
    )


def solution(mesh):
    tokens = P(("dp", "seq"), None)
    placed = (tokens,) * 6 + (P("dp", None),) + (P(),) * 4
    return jax.shard_map(
        shards,
        mesh=mesh,
        in_specs=placed,
        out_specs=(tokens,) * 3 + (P(None, "dp"),) * 4,
        check_vma=False,
    )
```

```python
import functools
import math

import jax
import jax.numpy as jnp
from jax import lax
from jax.experimental import pallas as pl
from jax.experimental.pallas import tpu as pltpu
from jax.sharding import PartitionSpec as P

H = 32
HD = 128
RANK = 8
ADAPTER_ALPHA = 16
SCALING = 1.0 / math.sqrt(HD)
LOG2E = 1.4426950408889634
BF16 = jnp.bfloat16
F32 = jnp.float32
NT = (((1,), (1,)), ((), ()))
MIB = 1024 * 1024
COST = pl.CostEstimate(flops=0, bytes_accessed=0, transcendentals=0)
ATTENTION_COST = pl.CostEstimate(flops=10**10, bytes_accessed=0, transcendentals=0)
LAST_HEADS = 2
LATE_OUT = 1
WHOLE_IN = (False, False)
WHOLE_OUT = (False, True)
ORDER = (6, 2, 4, 7, 3, 5, 1)
CHAIN = tuple((place, max(1, place - 3)) for place in range(1, 8))
PLAN = (
    ((6, 2, 4), ()),
    ((), ()),
    ((3, 5), ()),
    ((), ()),
    ((7,), (1,)),
)


def params(mebibytes):
    return pltpu.CompilerParams(vmem_limit_bytes=mebibytes * MIB)


def offsets_of(count):
    return (0,) + ORDER if count == 1 + len(ORDER) else tuple(range(count))


def pair_offsets(members):
    return [offset for offset in offsets_of(members) if offset % 2 == 0]


def part_of(refs, me, offset):
    if len(refs) == 1:
        return refs[0].at[me ^ offset]
    return refs[offsets_of(len(refs)).index(offset)]


def group_shapes(whole, members, shape, dtype):
    if whole:
        return [jax.ShapeDtypeStruct((members,) + shape, dtype)]
    return [jax.ShapeDtypeStruct(shape, dtype)] * members


def any_specs(count):
    return [pl.BlockSpec(memory_space=pl.ANY)] * count


def vmem_specs(count):
    return [pl.BlockSpec(memory_space=pltpu.VMEM)] * count


def dot_nt(left, right):
    return lax.dot_general(left, right, NT, preferred_element_type=F32)


def two_parts(value):
    high = value.astype(BF16)
    low = (value - high.astype(F32)).astype(BF16)
    return high, low


def three_parts(value):
    high, _ = two_parts(value)
    rest = value - high.astype(F32)
    middle, low = two_parts(rest)
    return high, middle, low


def side_rows(out, grad, hidden, downs):
    rows = out.shape[0]
    product = out.astype(F32) * grad.astype(F32)
    heads_at = lax.broadcasted_iota(jnp.int32, (H * HD, 128), 0) // HD
    lanes = lax.broadcasted_iota(jnp.int32, (H * HD, 128), 1)
    pick = jnp.where(heads_at == lanes, 1.0, 0.0).astype(BF16)
    split = jnp.concatenate(three_parts(product), axis=0)
    sums = jnp.dot(split, pick, preferred_element_type=F32)
    delta = (sums[:rows] + (sums[rows : 2 * rows] + sums[2 * rows :])).T[:H]
    return three_parts(delta), dot_nt(hidden, downs).T.astype(BF16)


def pack_kernel(members, heads_here, first_head, stage_heads, with_side, whole, *refs):
    refs = list(refs)
    sources = [refs.pop(0) for _ in range(4)]
    side_refs = [refs.pop(0) for _ in range(5 if with_side else 0)]
    messages = [refs.pop(0) for _ in range(1 if whole else members)]
    held, in_sems, out_sems = refs[:3]
    side_held, side_sems = refs[3:-1], refs[-1]
    me = lax.axis_index("seq")
    rows = sources[0].shape[0]
    reads = []
    for offset in range(members):
        target = me ^ offset
        for head in range(stage_heads):
            start = pl.multiple_of((target * heads_here + first_head + head) * HD, HD)
            for which in range(4):
                place = head * 4 + which
                reads.append(
                    pltpu.make_async_copy(
                        sources[which].at[:, pl.ds(start, HD)],
                        held.at[target, place * rows : (place + 1) * rows],
                        in_sems.at[offset, place],
                    )
                )
    bulk = 4 * stage_heads * rows

    def write(offset, low, count, sem):
        return pltpu.make_async_copy(
            held.at[me ^ offset, low : low + count],
            part_of(messages, me, offset).at[low : low + count],
            sem,
        )

    writes = [write(offset, 0, bulk, out_sems.at[0, offset]) for offset in range(members)]
    side_reads = [
        pltpu.make_async_copy(ref, there, side_sems.at[place])
        for place, (ref, there) in enumerate(zip(side_refs, side_held))
    ]
    for copy in reads + side_reads:
        copy.start()
    per_message = 4 * stage_heads
    for offset in range(members):
        for place in range(per_message):
            reads[offset * per_message + place].wait()
        writes[offset].start()
    if with_side:
        for copy in side_reads:
            copy.wait()
        out, grad, hidden, downq, downv = (there[...] for there in side_held)
        parts, lows = side_rows(out, grad, hidden, jnp.concatenate([downq, downv], axis=0))
        blank = jnp.zeros((16 - 3 * heads_here, rows), BF16)
        for member in range(members):
            here = slice(member * heads_here, (member + 1) * heads_here)
            held[member, bulk:] = jnp.concatenate(
                [part[here] for part in parts] + [blank, lows], axis=0
            )
        for offset in range(members):
            writes.append(write(offset, bulk, 32, out_sems.at[1, offset]))
            writes[-1].start()
    for copy in writes:
        copy.wait()


def pack(sources, side_sources, members, heads_here, first_head, stage_heads, whole):
    rows = sources[0].shape[0]
    shape = (4 * stage_heads * rows + (32 if side_sources else 0), HD)
    size = 2 * 4 * rows * stage_heads * HD * members * 2
    return pl.pallas_call(
        functools.partial(
            pack_kernel, members, heads_here, first_head, stage_heads, bool(side_sources), whole
        ),
        out_shape=group_shapes(whole, members, shape, BF16),
        in_specs=any_specs(4 + len(side_sources)),
        out_specs=any_specs(1 if whole else members),
        scratch_shapes=[
            pltpu.VMEM((members,) + shape, BF16),
            pltpu.SemaphoreType.DMA((members, 4 * stage_heads)),
            pltpu.SemaphoreType.DMA((2, members)),
        ]
        + [pltpu.VMEM(source.shape, BF16) for source in side_sources]
        + [pltpu.SemaphoreType.DMA((5,))],
        compiler_params=params(56),
        cost_estimate=COST,
        name="pack",
    )(*sources, *side_sources)


def begin_of(lengths_ref, positions):
    begin = jnp.int32(0) * positions
    start = jnp.int32(0)
    for index in range(lengths_ref.shape[1] - 1):
        start = start + lengths_ref[0, index]
        begin = jnp.where(positions >= start, start, begin)
    return begin


def attention_kernel(
    members,
    heads_here,
    first_head,
    stage_heads,
    counts,
    lengths_ref,
    upq_ref,
    upv_ref,
    cos_ref,
    sin_ref,
    *refs,
):
    refs = list(refs)
    messages, sides, outs, backs = [], [], [], []
    for group, count in zip((messages, sides), counts):
        group.extend(refs.pop(0) for _ in range(count))
    sides = sides or messages
    earlier_back = None if first_head == 0 else refs.pop(0)
    for group, count in zip((outs, backs), counts[2:]):
        group.extend(refs.pop(0) for _ in range(count))
    last = first_head + stage_heads == heads_here
    terms_ref = refs.pop(0)
    held, side_held, key_flip, grads, key_acc, value_acc, back_ref = refs[:7]
    in_sems, side_sems, out_sems = refs[7:]
    me = lax.axis_index("seq")
    side_low = sides[0].shape[-2] - 32
    rows = side_held.shape[1] // members
    total = rows * members
    block = min(256, total)
    reach = total // 2
    rows_of = [
        pl.ds(pl.multiple_of((me ^ offset) * rows, rows), rows) for offset in range(members)
    ]
    copies = []
    for offset in range(members):
        copies.append(
            pltpu.make_async_copy(
                part_of(messages, me, offset), held.at[me ^ offset], in_sems.at[offset]
            )
        )
        copies.append(
            pltpu.make_async_copy(
                part_of(sides, me, offset).at[side_low : side_low + 32],
                side_held.at[:, rows_of[offset]],
                side_sems.at[offset],
            )
        )
    for copy in copies:
        copy.start()
    key_acc[...] = jnp.zeros_like(key_acc)
    value_acc[...] = jnp.zeros_like(value_acc)
    terms_ref[...] = jnp.zeros_like(terms_ref)
    for copy in copies:
        copy.wait()
    columns = [slice(head * HD, (head + 1) * HD) for head in range(stage_heads)]

    def rows_at(place, low, count):
        first = low // rows
        taken = held[pl.ds(first, count // rows), place * rows : (place + 1) * rows, :]
        return taken.reshape(count, HD)

    for head in range(stage_heads):
        key_flip[head] = rows_at(4 * head + 1, 0, total).astype(F32).T.astype(BF16)

    def query_block(low, key_low, width):
        positions = low + lax.broadcasted_iota(jnp.int32, (1, block), 1)
        begin = begin_of(lengths_ref, positions)
        key_positions = key_low + lax.broadcasted_iota(jnp.int32, (width, block), 0)
        allowed = (key_positions >= begin) & (key_positions <= positions)
        bias = jnp.where(allowed, 0.0, -1e30).astype(F32)
        here = pl.ds(low, block)
        keys_here = pl.ds(key_low, width)
        cosine = cos_ref[:, here]
        sine = sin_ref[:, here]
        back_query = jnp.zeros((RANK, block), F32)
        parts = side_held[0:16, here].astype(F32)
        for head in range(stage_heads):
            cols = columns[head]
            query = rows_at(4 * head, low, block)
            grad = rows_at(4 * head + 3, low, block)
            scores = dot_nt(rows_at(4 * head + 1, key_low, width), query) + bias
            grad_prob = dot_nt(rows_at(4 * head + 2, key_low, width), grad)
            top = jnp.max(scores, axis=0, keepdims=True)
            weights = jnp.exp2((scores - top) * (SCALING * LOG2E))
            inverse = 1.0 / jnp.sum(weights, axis=0, keepdims=True)
            probs = weights * inverse
            row = first_head + head
            delta = sum(
                parts[place : place + 1] for place in range(row, 3 * heads_here, heads_here)
            )
            grad_score = (probs * (grad_prob - delta)).astype(BF16)
            value_acc[head, keys_here, :] += jnp.dot(
                probs.astype(BF16), grad, preferred_element_type=F32
            )
            key_acc[head, keys_here, :] += jnp.dot(grad_score, query, preferred_element_type=F32)
            flipped = SCALING * jnp.dot(
                key_flip[head, :, keys_here], grad_score, preferred_element_type=F32
            )
            grads[pl.ds(low // rows, block // rows), 0, :, cols] = (
                flipped.T.astype(BF16).reshape(block // rows, rows, HD)
            )
            rounded = flipped.astype(BF16).astype(F32)
            first = rounded[: HD // 2]
            second = rounded[HD // 2 :]
            before = jnp.concatenate(
                [first * cosine + second * sine, second * cosine - first * sine], axis=0
            ).astype(BF16)
            back_query += jnp.dot(upq_ref[:, cols], before, preferred_element_type=F32)
            terms_ref[0:RANK, cols] += dot_nt(side_held[16:24, here], before)
        back_ref[0:RANK, here] = back_query

    widths = [block + part * reach // 4 for part in range(5)]

    @pl.loop(0, total // block)
    def _(index):
        low = pl.multiple_of(index * block, block)
        needed = low + block - begin_of(lengths_ref, low)
        for place, width in enumerate(widths):
            fits = needed <= width
            if place:
                fits = fits & (needed > widths[place - 1])

            @pl.when(fits)
            def _(width=width):
                key_low = pl.multiple_of(jnp.maximum(low + block - width, 0), 128)
                query_block(low, key_low, width)

    back_value = jnp.zeros((RANK, total), F32)
    for head in range(stage_heads):
        cols = columns[head]
        grads[:, 1, :, cols] = (key_acc[head] * SCALING).astype(BF16).reshape(members, rows, HD)
        value_grad = value_acc[head].astype(BF16)
        grads[:, 2, :, cols] = value_grad.reshape(members, rows, HD)
        back_value += dot_nt(upv_ref[:, cols], value_grad)
        terms_ref[RANK : 2 * RANK, cols] = jnp.dot(
            side_held[24:32, :], value_grad, preferred_element_type=F32
        )
    back_ref[RANK : 2 * RANK, :] = back_value
    copies = [
        pltpu.make_async_copy(
            grads.at[me ^ offset], part_of(outs, me, offset), out_sems.at[offset]
        )
        for offset in range(members)
    ]
    for copy in copies:
        copy.start()
    back = back_ref[...]
    if earlier_back is not None:
        back = back + earlier_back[...]
    if last:
        back_ref[...] = back
        for out, offset in zip(backs, pair_offsets(members)):
            low = pl.multiple_of((me ^ offset) // 2 * 2 * rows, 2 * rows)
            out[...] = back_ref[:, pl.ds(low, 2 * rows)]
    else:
        backs[0][...] = back
    for copy in copies:
        copy.wait()


def attention(
    lengths,
    ups,
    turns,
    messages,
    sides,
    earlier_back,
    heads_here,
    first_head,
    stage_heads,
    members,
    rows,
    whole_out,
):
    total = rows * members
    width = stage_heads * HD
    last = first_head + stage_heads == heads_here
    out_shapes = group_shapes(whole_out, members, (3, rows, width), BF16)
    back_shapes = [jax.ShapeDtypeStruct((2 * RANK, total), F32)]
    if last:
        back_shapes = [jax.ShapeDtypeStruct((2 * RANK, 2 * rows), F32)] * (members // 2)
    earlier = [] if first_head == 0 else list(sides) + [earlier_back]
    counts = (len(messages), len(earlier[:-1]), len(out_shapes), len(back_shapes))
    results = pl.pallas_call(
        functools.partial(attention_kernel, members, heads_here, first_head, stage_heads, counts),
        out_shape=out_shapes + back_shapes + [jax.ShapeDtypeStruct((2 * RANK, width), F32)],
        in_specs=[pl.BlockSpec(memory_space=pltpu.SMEM)]
        + vmem_specs(4)
        + any_specs(len(messages))
        + (any_specs(len(sides)) + vmem_specs(1) if earlier else []),
        out_specs=any_specs(len(out_shapes)) + vmem_specs(len(back_shapes) + 1),
        scratch_shapes=[
            pltpu.VMEM((members,) + messages[0].shape[-2:], BF16),
            pltpu.VMEM((32, total), BF16),
            pltpu.VMEM((stage_heads, HD, total), BF16),
            pltpu.VMEM((members, 3, rows, width), BF16),
            pltpu.VMEM((stage_heads, total, HD), F32),
            pltpu.VMEM((stage_heads, total, HD), F32),
            pltpu.VMEM((2 * RANK, total), F32),
            pltpu.SemaphoreType.DMA((members,)),
            pltpu.SemaphoreType.DMA((members,)),
            pltpu.SemaphoreType.DMA((members,)),
        ],
        compiler_params=params(32),
        cost_estimate=ATTENTION_COST,
        name="attention",
    )(lengths, *ups, *turns, *messages, *earlier)
    split = len(out_shapes)
    return results[:split], results[split:-1], results[-1]


def small_call(kernel, out_shape, *operands, mebibytes=4, name="sum"):
    outs = len(out_shape) if isinstance(out_shape, list) else 1
    return pl.pallas_call(
        kernel,
        out_shape=out_shape,
        in_specs=vmem_specs(len(operands)),
        out_specs=vmem_specs(outs) if isinstance(out_shape, list) else vmem_specs(1)[0],
        compiler_params=params(mebibytes),
        cost_estimate=COST,
        name=name,
    )(*operands)


def total_of(refs):
    total = refs[0][...]
    for ref in refs[1:]:
        total = total + ref[...]
    return total


def fold(tiles, ups):
    def kernel(*refs):
        out = refs[-1]
        low = refs[0].shape[1]
        out[:, :low] = total_of(refs[: len(tiles)])
        for up in refs[len(tiles) : -1]:
            out[:, low : low + up.shape[1]] = up[...]
            low += up.shape[1]

    width = tiles[0].shape[1] + sum(up.shape[1] for up in ups)
    shape = jax.ShapeDtypeStruct((2 * RANK, width), F32)
    return small_call(kernel, shape, *tiles, *ups, name="fold")


def down_kernel(members, packs, own_ref, other_ref, hidden_ref, beside_ref, *refs):
    messages = refs[:packs]
    held, sems = refs[packs:]
    me = lax.axis_index("seq")
    pack_here = lax.axis_index("dp")
    first_core = me % 2 == 0
    rows = hidden_ref.shape[0]

    def half(value):
        return jnp.where(first_core, value[:RANK], value[RANK:])

    own, other = half(own_ref[...]), half(other_ref[...])
    back = own[:, : 2 * rows] + other[:, : 2 * rows]
    here = jnp.where(first_core, back[:, :rows], back[:, rows:]).astype(BF16)
    there = jnp.where(first_core, back[:, rows:], back[:, :rows]).astype(BF16)
    terms = jnp.dot(here, hidden_ref[...], preferred_element_type=F32) + jnp.dot(
        there, beside_ref[...], preferred_element_type=F32
    )
    own_up, other_up = own[:, 2 * rows :], other[:, 2 * rows :]
    ups = jnp.concatenate(
        [jnp.where(first_core, own_up, other_up), jnp.where(first_core, other_up, own_up)], axis=1
    )
    down_cols = terms.shape[1] // packs
    sharers = members // packs
    for target in range(packs):
        held[target, :, :down_cols] = terms[:, target * down_cols : (target + 1) * down_cols]
        held[target, :, down_cols:] = jnp.where(me // sharers == target, ups, 0.0)
    copies = [
        pltpu.make_async_copy(held.at[pack_here ^ offset], messages[offset], sems.at[offset])
        for offset in range(packs)
    ]
    for copy in copies:
        copy.start()
    for copy in copies:
        copy.wait()


def down_terms(own, other, hidden, beside, members, packs):
    rows = hidden.shape[0]
    width = hidden.shape[1] // packs + 2 * (own.shape[1] - 2 * rows)
    return pl.pallas_call(
        functools.partial(down_kernel, members, packs),
        out_shape=[jax.ShapeDtypeStruct((RANK, width), F32)] * packs,
        in_specs=vmem_specs(4),
        out_specs=any_specs(packs),
        scratch_shapes=[
            pltpu.VMEM((packs, RANK, width), F32),
            pltpu.SemaphoreType.DMA((packs,)),
        ],
        compiler_params=params(8),
        cost_estimate=COST,
        name="down_terms",
    )(own, other, hidden, beside)


def sum_packs(pieces, sharing_chips, down_cols):
    size = pieces[0].shape[1] - down_cols

    def kernel(*refs):
        out = refs[-1]
        me = lax.axis_index("seq")
        total = total_of(refs[:-1])
        out[:, :down_cols] = total[:, :down_cols]
        for place in range(sharing_chips):
            low = down_cols + place * size
            mine = (me // 2) % sharing_chips == place
            out[:, low : low + size] = jnp.where(mine, total[:, down_cols:], 0.0)

    shape = jax.ShapeDtypeStruct((RANK, down_cols + sharing_chips * size), F32)
    return small_call(kernel, shape, *pieces, name="sum_packs")


def sum_chips(pieces):
    def kernel(*refs):
        refs[-1][...] = total_of(refs[:-1]) * (ADAPTER_ALPHA / RANK)

    shape = jax.ShapeDtypeStruct(pieces[0].shape, F32)
    return small_call(kernel, shape, *pieces, name="sum_chips")


def finish(own, other, down_cols):
    def kernel(own_ref, other_ref, *outs):
        first_core = lax.axis_index("seq") % 2 == 0
        mine, beside = own_ref[...], other_ref[...]
        query = jnp.where(first_core, mine, beside)
        value = jnp.where(first_core, beside, mine)
        outs[0][...] = query[:, :down_cols]
        outs[1][...] = query[:, down_cols:]
        outs[2][...] = value[:, :down_cols]
        outs[3][...] = value[:, down_cols:]

    up_cols = own.shape[1] - down_cols
    shapes = [jax.ShapeDtypeStruct((RANK, cols), F32) for cols in (down_cols, up_cols)] * 2
    return small_call(kernel, shapes, own, other, name="finish")


def unpack_kernel(members, heads_here, stages, counts, *refs):
    count = sum(counts)
    groups = [refs[sum(counts[:i]) : sum(counts[: i + 1])] for i in range(len(counts))]
    outs = refs[count : count + 3]
    held = refs[count + 3 : count + 3 + len(stages)]
    in_sems, out_sems = refs[count + 3 + len(stages) :]
    me = lax.axis_index("seq")
    reads = []
    writes = []
    for stage, (first_head, stage_heads) in enumerate(stages):
        for offset in range(members):
            source = me ^ offset
            start = pl.multiple_of((source * heads_here + first_head) * HD, HD)
            reads.append(
                pltpu.make_async_copy(
                    part_of(groups[stage], me, offset),
                    held[stage].at[offset],
                    in_sems.at[stage, offset],
                )
            )
            writes.append(
                [
                    pltpu.make_async_copy(
                        held[stage].at[offset, which],
                        outs[which].at[:, pl.ds(start, stage_heads * HD)],
                        out_sems.at[stage, offset, which],
                    )
                    for which in range(3)
                ]
            )
    for copy in reads:
        copy.start()
    for copy, followers in zip(reads, writes):
        copy.wait()
        for follower in followers:
            follower.start()
    for followers in writes:
        for follower in followers:
            follower.wait()


def unpack(groups, members, heads_here, stages):
    rows = groups[0][0].shape[-2]
    counts = [len(group) for group in groups]
    messages = [message for group in groups for message in group]
    width = members * heads_here * HD
    return pl.pallas_call(
        functools.partial(unpack_kernel, members, heads_here, stages, counts),
        out_shape=[jax.ShapeDtypeStruct((rows, width), BF16)] * 3,
        in_specs=any_specs(len(messages)),
        out_specs=any_specs(3),
        scratch_shapes=[
            pltpu.VMEM((members, 3, rows, stage_heads * HD), BF16) for _, stage_heads in stages
        ]
        + [
            pltpu.SemaphoreType.DMA((len(stages), members)),
            pltpu.SemaphoreType.DMA((len(stages), members, 3)),
        ],
        compiler_params=params(56),
        cost_estimate=COST,
        name="unpack",
    )(*messages)


def exchange(messages, axis):
    count = len(messages)
    if count == 1:
        return [lax.all_to_all(messages[0], axis, split_axis=0, concat_axis=0, tiled=True)]
    return [
        lax.ppermute(message, axis, [(i, i ^ offset) for i in range(count)]) if offset else message
        for offset, message in zip(offsets_of(count), messages)
    ]


def turn_tables(lengths_row, total):
    positions = jnp.arange(total, dtype=jnp.int32)
    ends = jnp.cumsum(lengths_row)
    starts = ends - lengths_row
    begin = jnp.max(jnp.where(positions[:, None] >= starts[None, :], starts[None, :], 0), axis=1)
    half = HD // 2
    inverse = jnp.exp(-(jnp.arange(half, dtype=F32) * (2.0 / HD)) * math.log(10000.0))
    angles = inverse[:, None] * (positions - begin).astype(F32)[None, :]
    return jnp.cos(angles), jnp.sin(angles)


def shards(
    hidden,
    queries,
    key_states,
    value_states,
    attention_out,
    grad_out,
    lengths,
    down_query,
    up_query,
    down_value,
    up_value,
):
    rows = queries.shape[0]
    members = lax.axis_size("seq")
    packs = lax.axis_size("dp")
    total = rows * members
    heads_here = H // members
    stages = [(0, heads_here)]
    if heads_here > 1:
        stages = [(0, heads_here - LAST_HEADS), (heads_here - LAST_HEADS, LAST_HEADS)]
    sources = (queries, key_states, value_states, grad_out)
    me = lax.axis_index("seq")

    side_sources = (attention_out, grad_out, hidden, down_query, down_value)
    turns = turn_tables(lengths[0], total)
    beside = lax.ppermute(hidden, "seq", [(i, i ^ 1) for i in range(members)])
    packed = []
    for (first_head, stage_heads), whole in zip(stages, WHOLE_IN):
        extra = () if packed else side_sources
        held_back = sources
        if packed:
            held_back, _, beside = lax.optimization_barrier((sources, packed[0][0], beside))
        packed.append(
            list(pack(held_back, extra, members, heads_here, first_head, stage_heads, whole))
        )
    arrived = []
    home = []
    ups = []
    back = [None]
    planned = len(stages) == 2 and members == 8

    def after(value, stage, offsets):
        if not planned or not offsets:
            return value
        places = [offsets_of(members).index(offset) for offset in offsets]
        if len(home[stage]) == 1:
            places = [0]
        taken = tuple(home[stage][place] for place in places)
        value, taken = lax.optimization_barrier((value, taken))
        for place, message in zip(places, taken):
            home[stage][place] = message
        return value

    for index, (first_head, stage_heads) in enumerate(stages):
        arrived.append(exchange(packed[index], "seq"))
        if planned and index == 0:
            for place, before in CHAIN:
                packed[1][place], arrived[0][before] = lax.optimization_barrier(
                    (packed[1][place], arrived[0][before])
                )
        start = (me * heads_here + first_head) * HD
        up_here = tuple(
            lax.dynamic_slice_in_dim(up, start, stage_heads * HD, 1) for up in (up_query, up_value)
        )
        grads, back, up_terms = attention(
            lengths,
            up_here,
            turns,
            arrived[index],
            arrived[0],
            back[0],
            heads_here,
            first_head,
            stage_heads,
            members,
            rows,
            WHOLE_OUT[index],
        )
        back = list(back)
        home.append(list(grads) if index else exchange(grads, "seq"))
        ups.append(up_terms)
    home_early = not (planned and len(home[-1]) == 1)
    if len(home) > 1 and home_early:
        home[1] = exchange(home[1], "seq")

    def swap(value, offset):
        return lax.ppermute(value, "seq", [(i, i ^ offset) for i in range(members)])

    def planned_after(value, place):
        return after(after(value, 0, PLAN[place][0]), 1, PLAN[place][1])

    back = planned_after(list(back), 0)
    tiles = [
        swap(tile, offset) if offset else tile
        for offset, tile in zip(pair_offsets(members), back)
    ]
    own = planned_after(fold(tiles, ups), 1)
    if not home_early and LATE_OUT == -1:
        own, home[1][0] = lax.optimization_barrier((own, home[1][0]))
    other = planned_after(swap(own, 1), 2)
    if not home_early and LATE_OUT == 0:
        other, home[1][0] = lax.optimization_barrier((other, home[1][0]))
    pieces = list(down_terms(own, other, hidden, beside, members, packs))
    if not home_early and LATE_OUT == 1:
        pieces[0], home[1][0] = lax.optimization_barrier((pieces[0], home[1][0]))
    if not home_early:
        home[1] = exchange(home[1], "seq")
    pieces = exchange(pieces, "dp")
    down_cols = hidden.shape[1] // packs
    summed = planned_after(sum_packs(pieces, members // packs // 2, down_cols), 3)
    if members == 8:
        pieces = [swap(summed, offset) if offset else summed for offset in pair_offsets(members)]
    else:
        step = 2
        while step < members // 2:
            summed = summed + swap(summed, step)
            step *= 2
        pieces = [summed, swap(summed, step)]
    summed = planned_after(sum_chips(pieces), 4)
    down_query_grad, up_query_grad, down_value_grad, up_value_grad = finish(
        summed, swap(summed, 1), down_cols
    )
    grad_queries, grad_keys, value_gradients = unpack(home, members, heads_here, stages)
    return (
        grad_queries,
        grad_keys,
        value_gradients,
        down_query_grad,
        up_query_grad,
        down_value_grad,
        up_value_grad,
    )


def solution(mesh):
    tokens = P(("dp", "seq"), None)
    placed = (tokens,) * 6 + (P("dp", None),) + (P(),) * 4
    return jax.shard_map(
        shards,
        mesh=mesh,
        in_specs=placed,
        out_specs=(tokens,) * 3 + (P(None, "dp"),) * 4,
        check_vma=False,
    )
```

```python
import functools
import math

import jax
import jax.numpy as jnp
from jax import lax
from jax.experimental import pallas as pl
from jax.experimental.pallas import tpu as pltpu
from jax.sharding import PartitionSpec as P

H = 32
HD = 128
RANK = 8
ADAPTER_ALPHA = 16
SCALING = 1.0 / math.sqrt(HD)
LOG2E = 1.4426950408889634
BF16 = jnp.bfloat16
F32 = jnp.float32
NT = (((1,), (1,)), ((), ()))
MIB = 1024 * 1024
COST = pl.CostEstimate(flops=0, bytes_accessed=0, transcendentals=0)
ATTENTION_COST = pl.CostEstimate(flops=10**10, bytes_accessed=0, transcendentals=0)
LAST_HEADS = 2
LATE_OUT = 1
WHOLE_IN = (False, False)
WHOLE_OUT = (False, True)
ORDER = (6, 2, 4, 3, 5, 7, 1)
CHAIN = tuple((place, max(1, place - 3)) for place in range(1, 8))
PLAN = (
    ((6, 2, 4), ()),
    ((), ()),
    ((3, 5), ()),
    ((), ()),
    ((7, 1), (1,)),
)


def params(mebibytes):
    return pltpu.CompilerParams(vmem_limit_bytes=mebibytes * MIB)


def offsets_of(count):
    return (0,) + ORDER if count == 1 + len(ORDER) else tuple(range(count))


def pair_offsets(members):
    return [offset for offset in offsets_of(members) if offset % 2 == 0]


def part_of(refs, me, offset):
    if len(refs) == 1:
        return refs[0].at[me ^ offset]
    return refs[offsets_of(len(refs)).index(offset)]


def group_shapes(whole, members, shape, dtype):
    if whole:
        return [jax.ShapeDtypeStruct((members,) + shape, dtype)]
    return [jax.ShapeDtypeStruct(shape, dtype)] * members


def any_specs(count):
    return [pl.BlockSpec(memory_space=pl.ANY)] * count


def vmem_specs(count):
    return [pl.BlockSpec(memory_space=pltpu.VMEM)] * count


def dot_nt(left, right):
    return lax.dot_general(left, right, NT, preferred_element_type=F32)


def two_parts(value):
    high = value.astype(BF16)
    low = (value - high.astype(F32)).astype(BF16)
    return high, low


def three_parts(value):
    high, _ = two_parts(value)
    rest = value - high.astype(F32)
    middle, low = two_parts(rest)
    return high, middle, low


def side_rows(out, grad, hidden, downs):
    rows = out.shape[0]
    product = out.astype(F32) * grad.astype(F32)
    heads_at = lax.broadcasted_iota(jnp.int32, (H * HD, 128), 0) // HD
    lanes = lax.broadcasted_iota(jnp.int32, (H * HD, 128), 1)
    pick = jnp.where(heads_at == lanes, 1.0, 0.0).astype(BF16)
    split = jnp.concatenate(three_parts(product), axis=0)
    sums = jnp.dot(split, pick, preferred_element_type=F32)
    delta = (sums[:rows] + (sums[rows : 2 * rows] + sums[2 * rows :])).T[:H]
    return three_parts(delta), dot_nt(hidden, downs).T.astype(BF16)


def pack_kernel(members, heads_here, first_head, stage_heads, with_side, whole, *refs):
    refs = list(refs)
    sources = [refs.pop(0) for _ in range(4)]
    side_refs = [refs.pop(0) for _ in range(5 if with_side else 0)]
    messages = [refs.pop(0) for _ in range(1 if whole else members)]
    held, in_sems, out_sems = refs[:3]
    side_held, side_sems = refs[3:-1], refs[-1]
    me = lax.axis_index("seq")
    rows = sources[0].shape[0]
    reads = []
    for offset in range(members):
        target = me ^ offset
        for head in range(stage_heads):
            start = pl.multiple_of((target * heads_here + first_head + head) * HD, HD)
            for which in range(4):
                place = head * 4 + which
                reads.append(
                    pltpu.make_async_copy(
                        sources[which].at[:, pl.ds(start, HD)],
                        held.at[target, place * rows : (place + 1) * rows],
                        in_sems.at[offset, place],
                    )
                )
    bulk = 4 * stage_heads * rows

    def write(offset, low, count, sem):
        return pltpu.make_async_copy(
            held.at[me ^ offset, low : low + count],
            part_of(messages, me, offset).at[low : low + count],
            sem,
        )

    writes = [write(offset, 0, bulk, out_sems.at[0, offset]) for offset in range(members)]
    side_reads = [
        pltpu.make_async_copy(ref, there, side_sems.at[place])
        for place, (ref, there) in enumerate(zip(side_refs, side_held))
    ]
    for copy in reads + side_reads:
        copy.start()
    per_message = 4 * stage_heads
    for offset in range(members):
        for place in range(per_message):
            reads[offset * per_message + place].wait()
        writes[offset].start()
    if with_side:
        for copy in side_reads:
            copy.wait()
        out, grad, hidden, downq, downv = (there[...] for there in side_held)
        parts, lows = side_rows(out, grad, hidden, jnp.concatenate([downq, downv], axis=0))
        blank = jnp.zeros((16 - 3 * heads_here, rows), BF16)
        for member in range(members):
            here = slice(member * heads_here, (member + 1) * heads_here)
            held[member, bulk:] = jnp.concatenate(
                [part[here] for part in parts] + [blank, lows], axis=0
            )
        for offset in range(members):
            writes.append(write(offset, bulk, 32, out_sems.at[1, offset]))
            writes[-1].start()
    for copy in writes:
        copy.wait()


def pack(sources, side_sources, members, heads_here, first_head, stage_heads, whole):
    rows = sources[0].shape[0]
    shape = (4 * stage_heads * rows + (32 if side_sources else 0), HD)
    size = 2 * 4 * rows * stage_heads * HD * members * 2
    return pl.pallas_call(
        functools.partial(
            pack_kernel, members, heads_here, first_head, stage_heads, bool(side_sources), whole
        ),
        out_shape=group_shapes(whole, members, shape, BF16),
        in_specs=any_specs(4 + len(side_sources)),
        out_specs=any_specs(1 if whole else members),
        scratch_shapes=[
            pltpu.VMEM((members,) + shape, BF16),
            pltpu.SemaphoreType.DMA((members, 4 * stage_heads)),
            pltpu.SemaphoreType.DMA((2, members)),
        ]
        + [pltpu.VMEM(source.shape, BF16) for source in side_sources]
        + [pltpu.SemaphoreType.DMA((5,))],
        compiler_params=params(56),
        cost_estimate=COST,
        name="pack",
    )(*sources, *side_sources)


def begin_of(lengths_ref, positions):
    begin = jnp.int32(0) * positions
    start = jnp.int32(0)
    for index in range(lengths_ref.shape[1] - 1):
        start = start + lengths_ref[0, index]
        begin = jnp.where(positions >= start, start, begin)
    return begin


def attention_kernel(
    members,
    heads_here,
    first_head,
    stage_heads,
    counts,
    lengths_ref,
    upq_ref,
    upv_ref,
    cos_ref,
    sin_ref,
    *refs,
):
    refs = list(refs)
    messages, sides, outs, backs = [], [], [], []
    for group, count in zip((messages, sides), counts):
        group.extend(refs.pop(0) for _ in range(count))
    sides = sides or messages
    earlier_back = None if first_head == 0 else refs.pop(0)
    for group, count in zip((outs, backs), counts[2:]):
        group.extend(refs.pop(0) for _ in range(count))
    last = first_head + stage_heads == heads_here
    terms_ref = refs.pop(0)
    held, side_held, key_flip, grads, key_acc, value_acc, back_ref = refs[:7]
    in_sems, side_sems, out_sems = refs[7:]
    me = lax.axis_index("seq")
    side_low = sides[0].shape[-2] - 32
    rows = side_held.shape[1] // members
    total = rows * members
    block = min(256, total)
    reach = total // 2
    rows_of = [
        pl.ds(pl.multiple_of((me ^ offset) * rows, rows), rows) for offset in range(members)
    ]
    copies = []
    for offset in range(members):
        copies.append(
            pltpu.make_async_copy(
                part_of(messages, me, offset), held.at[me ^ offset], in_sems.at[offset]
            )
        )
        copies.append(
            pltpu.make_async_copy(
                part_of(sides, me, offset).at[side_low : side_low + 32],
                side_held.at[:, rows_of[offset]],
                side_sems.at[offset],
            )
        )
    for copy in copies:
        copy.start()
    key_acc[...] = jnp.zeros_like(key_acc)
    value_acc[...] = jnp.zeros_like(value_acc)
    terms_ref[...] = jnp.zeros_like(terms_ref)
    for copy in copies:
        copy.wait()
    columns = [slice(head * HD, (head + 1) * HD) for head in range(stage_heads)]

    def rows_at(place, low, count):
        first = low // rows
        taken = held[pl.ds(first, count // rows), place * rows : (place + 1) * rows, :]
        return taken.reshape(count, HD)

    for head in range(stage_heads):
        key_flip[head] = rows_at(4 * head + 1, 0, total).astype(F32).T.astype(BF16)

    def query_block(low, key_low, width):
        positions = low + lax.broadcasted_iota(jnp.int32, (1, block), 1)
        begin = begin_of(lengths_ref, positions)
        key_positions = key_low + lax.broadcasted_iota(jnp.int32, (width, block), 0)
        allowed = (key_positions >= begin) & (key_positions <= positions)
        bias = jnp.where(allowed, 0.0, -1e30).astype(F32)
        here = pl.ds(low, block)
        keys_here = pl.ds(key_low, width)
        cosine = cos_ref[:, here]
        sine = sin_ref[:, here]
        back_query = jnp.zeros((RANK, block), F32)
        parts = side_held[0:16, here].astype(F32)
        for head in range(stage_heads):
            cols = columns[head]
            query = rows_at(4 * head, low, block)
            grad = rows_at(4 * head + 3, low, block)
            scores = dot_nt(rows_at(4 * head + 1, key_low, width), query) + bias
            grad_prob = dot_nt(rows_at(4 * head + 2, key_low, width), grad)
            top = jnp.max(scores, axis=0, keepdims=True)
            weights = jnp.exp2((scores - top) * (SCALING * LOG2E))
            inverse = 1.0 / jnp.sum(weights, axis=0, keepdims=True)
            probs = weights * inverse
            row = first_head + head
            delta = sum(
                parts[place : place + 1] for place in range(row, 3 * heads_here, heads_here)
            )
            grad_score = (probs * (grad_prob - delta)).astype(BF16)
            value_acc[head, keys_here, :] += jnp.dot(
                probs.astype(BF16), grad, preferred_element_type=F32
            )
            key_acc[head, keys_here, :] += jnp.dot(grad_score, query, preferred_element_type=F32)
            flipped = SCALING * jnp.dot(
                key_flip[head, :, keys_here], grad_score, preferred_element_type=F32
            )
            grads[pl.ds(low // rows, block // rows), 0, :, cols] = (
                flipped.T.astype(BF16).reshape(block // rows, rows, HD)
            )
            rounded = flipped.astype(BF16).astype(F32)
            first = rounded[: HD // 2]
            second = rounded[HD // 2 :]
            before = jnp.concatenate(
                [first * cosine + second * sine, second * cosine - first * sine], axis=0
            ).astype(BF16)
            back_query += jnp.dot(upq_ref[:, cols], before, preferred_element_type=F32)
            terms_ref[0:RANK, cols] += dot_nt(side_held[16:24, here], before)
        back_ref[0:RANK, here] = back_query

    widths = [block + part * reach // 4 for part in range(5)]

    @pl.loop(0, total // block)
    def _(index):
        low = pl.multiple_of(index * block, block)
        needed = low + block - begin_of(lengths_ref, low)
        for place, width in enumerate(widths):
            fits = needed <= width
            if place:
                fits = fits & (needed > widths[place - 1])

            @pl.when(fits)
            def _(width=width):
                key_low = pl.multiple_of(jnp.maximum(low + block - width, 0), 128)
                query_block(low, key_low, width)

    back_value = jnp.zeros((RANK, total), F32)
    for head in range(stage_heads):
        cols = columns[head]
        grads[:, 1, :, cols] = (key_acc[head] * SCALING).astype(BF16).reshape(members, rows, HD)
        value_grad = value_acc[head].astype(BF16)
        grads[:, 2, :, cols] = value_grad.reshape(members, rows, HD)
        back_value += dot_nt(upv_ref[:, cols], value_grad)
        terms_ref[RANK : 2 * RANK, cols] = jnp.dot(
            side_held[24:32, :], value_grad, preferred_element_type=F32
        )
    back_ref[RANK : 2 * RANK, :] = back_value
    copies = [
        pltpu.make_async_copy(
            grads.at[me ^ offset], part_of(outs, me, offset), out_sems.at[offset]
        )
        for offset in range(members)
    ]
    for copy in copies:
        copy.start()
    back = back_ref[...]
    if earlier_back is not None:
        back = back + earlier_back[...]
    if last:
        back_ref[...] = back
        for out, offset in zip(backs, pair_offsets(members)):
            low = pl.multiple_of((me ^ offset) // 2 * 2 * rows, 2 * rows)
            out[...] = back_ref[:, pl.ds(low, 2 * rows)]
    else:
        backs[0][...] = back
    for copy in copies:
        copy.wait()


def attention(
    lengths,
    ups,
    turns,
    messages,
    sides,
    earlier_back,
    heads_here,
    first_head,
    stage_heads,
    members,
    rows,
    whole_out,
):
    total = rows * members
    width = stage_heads * HD
    last = first_head + stage_heads == heads_here
    out_shapes = group_shapes(whole_out, members, (3, rows, width), BF16)
    back_shapes = [jax.ShapeDtypeStruct((2 * RANK, total), F32)]
    if last:
        back_shapes = [jax.ShapeDtypeStruct((2 * RANK, 2 * rows), F32)] * (members // 2)
    earlier = [] if first_head == 0 else list(sides) + [earlier_back]
    counts = (len(messages), len(earlier[:-1]), len(out_shapes), len(back_shapes))
    results = pl.pallas_call(
        functools.partial(attention_kernel, members, heads_here, first_head, stage_heads, counts),
        out_shape=out_shapes + back_shapes + [jax.ShapeDtypeStruct((2 * RANK, width), F32)],
        in_specs=[pl.BlockSpec(memory_space=pltpu.SMEM)]
        + vmem_specs(4)
        + any_specs(len(messages))
        + (any_specs(len(sides)) + vmem_specs(1) if earlier else []),
        out_specs=any_specs(len(out_shapes)) + vmem_specs(len(back_shapes) + 1),
        scratch_shapes=[
            pltpu.VMEM((members,) + messages[0].shape[-2:], BF16),
            pltpu.VMEM((32, total), BF16),
            pltpu.VMEM((stage_heads, HD, total), BF16),
            pltpu.VMEM((members, 3, rows, width), BF16),
            pltpu.VMEM((stage_heads, total, HD), F32),
            pltpu.VMEM((stage_heads, total, HD), F32),
            pltpu.VMEM((2 * RANK, total), F32),
            pltpu.SemaphoreType.DMA((members,)),
            pltpu.SemaphoreType.DMA((members,)),
            pltpu.SemaphoreType.DMA((members,)),
        ],
        compiler_params=params(32),
        cost_estimate=ATTENTION_COST,
        name="attention",
    )(lengths, *ups, *turns, *messages, *earlier)
    split = len(out_shapes)
    return results[:split], results[split:-1], results[-1]


def small_call(kernel, out_shape, *operands, mebibytes=4, name="sum"):
    outs = len(out_shape) if isinstance(out_shape, list) else 1
    return pl.pallas_call(
        kernel,
        out_shape=out_shape,
        in_specs=vmem_specs(len(operands)),
        out_specs=vmem_specs(outs) if isinstance(out_shape, list) else vmem_specs(1)[0],
        compiler_params=params(mebibytes),
        cost_estimate=COST,
        name=name,
    )(*operands)


def total_of(refs):
    total = refs[0][...]
    for ref in refs[1:]:
        total = total + ref[...]
    return total


def fold(tiles, ups):
    def kernel(*refs):
        out = refs[-1]
        low = refs[0].shape[1]
        out[:, :low] = total_of(refs[: len(tiles)])
        for up in refs[len(tiles) : -1]:
            out[:, low : low + up.shape[1]] = up[...]
            low += up.shape[1]

    width = tiles[0].shape[1] + sum(up.shape[1] for up in ups)
    shape = jax.ShapeDtypeStruct((2 * RANK, width), F32)
    return small_call(kernel, shape, *tiles, *ups, name="fold")


def down_kernel(members, packs, own_ref, other_ref, hidden_ref, beside_ref, *refs):
    messages = refs[:packs]
    held, sems = refs[packs:]
    me = lax.axis_index("seq")
    pack_here = lax.axis_index("dp")
    first_core = me % 2 == 0
    rows = hidden_ref.shape[0]

    def half(value):
        return jnp.where(first_core, value[:RANK], value[RANK:])

    own, other = half(own_ref[...]), half(other_ref[...])
    back = own[:, : 2 * rows] + other[:, : 2 * rows]
    here = jnp.where(first_core, back[:, :rows], back[:, rows:]).astype(BF16)
    there = jnp.where(first_core, back[:, rows:], back[:, :rows]).astype(BF16)
    terms = jnp.dot(here, hidden_ref[...], preferred_element_type=F32) + jnp.dot(
        there, beside_ref[...], preferred_element_type=F32
    )
    own_up, other_up = own[:, 2 * rows :], other[:, 2 * rows :]
    ups = jnp.concatenate(
        [jnp.where(first_core, own_up, other_up), jnp.where(first_core, other_up, own_up)], axis=1
    )
    down_cols = terms.shape[1] // packs
    sharers = members // packs
    for target in range(packs):
        held[target, :, :down_cols] = terms[:, target * down_cols : (target + 1) * down_cols]
        held[target, :, down_cols:] = jnp.where(me // sharers == target, ups, 0.0)
    copies = [
        pltpu.make_async_copy(held.at[pack_here ^ offset], messages[offset], sems.at[offset])
        for offset in range(packs)
    ]
    for copy in copies:
        copy.start()
    for copy in copies:
        copy.wait()


def down_terms(own, other, hidden, beside, members, packs):
    rows = hidden.shape[0]
    width = hidden.shape[1] // packs + 2 * (own.shape[1] - 2 * rows)
    return pl.pallas_call(
        functools.partial(down_kernel, members, packs),
        out_shape=[jax.ShapeDtypeStruct((RANK, width), F32)] * packs,
        in_specs=vmem_specs(4),
        out_specs=any_specs(packs),
        scratch_shapes=[
            pltpu.VMEM((packs, RANK, width), F32),
            pltpu.SemaphoreType.DMA((packs,)),
        ],
        compiler_params=params(8),
        cost_estimate=COST,
        name="down_terms",
    )(own, other, hidden, beside)


def sum_packs(pieces, sharing_chips, down_cols):
    size = pieces[0].shape[1] - down_cols

    def kernel(*refs):
        out = refs[-1]
        me = lax.axis_index("seq")
        total = total_of(refs[:-1])
        out[:, :down_cols] = total[:, :down_cols]
        for place in range(sharing_chips):
            low = down_cols + place * size
            mine = (me // 2) % sharing_chips == place
            out[:, low : low + size] = jnp.where(mine, total[:, down_cols:], 0.0)

    shape = jax.ShapeDtypeStruct((RANK, down_cols + sharing_chips * size), F32)
    return small_call(kernel, shape, *pieces, name="sum_packs")


def sum_chips(pieces):
    def kernel(*refs):
        refs[-1][...] = total_of(refs[:-1]) * (ADAPTER_ALPHA / RANK)

    shape = jax.ShapeDtypeStruct(pieces[0].shape, F32)
    return small_call(kernel, shape, *pieces, name="sum_chips")


def finish(own, other, down_cols):
    def kernel(own_ref, other_ref, *outs):
        first_core = lax.axis_index("seq") % 2 == 0
        mine, beside = own_ref[...], other_ref[...]
        query = jnp.where(first_core, mine, beside)
        value = jnp.where(first_core, beside, mine)
        outs[0][...] = query[:, :down_cols]
        outs[1][...] = query[:, down_cols:]
        outs[2][...] = value[:, :down_cols]
        outs[3][...] = value[:, down_cols:]

    up_cols = own.shape[1] - down_cols
    shapes = [jax.ShapeDtypeStruct((RANK, cols), F32) for cols in (down_cols, up_cols)] * 2
    return small_call(kernel, shapes, own, other, name="finish")


def unpack_kernel(members, heads_here, stages, counts, *refs):
    count = sum(counts)
    groups = [refs[sum(counts[:i]) : sum(counts[: i + 1])] for i in range(len(counts))]
    outs = refs[count : count + 3]
    held = refs[count + 3 : count + 3 + len(stages)]
    in_sems, out_sems = refs[count + 3 + len(stages) :]
    me = lax.axis_index("seq")
    reads = []
    writes = []
    for stage, (first_head, stage_heads) in enumerate(stages):
        for offset in range(members):
            source = me ^ offset
            start = pl.multiple_of((source * heads_here + first_head) * HD, HD)
            reads.append(
                pltpu.make_async_copy(
                    part_of(groups[stage], me, offset),
                    held[stage].at[offset],
                    in_sems.at[stage, offset],
                )
            )
            writes.append(
                [
                    pltpu.make_async_copy(
                        held[stage].at[offset, which],
                        outs[which].at[:, pl.ds(start, stage_heads * HD)],
                        out_sems.at[stage, offset, which],
                    )
                    for which in range(3)
                ]
            )
    for copy in reads:
        copy.start()
    for copy, followers in zip(reads, writes):
        copy.wait()
        for follower in followers:
            follower.start()
    for followers in writes:
        for follower in followers:
            follower.wait()


def unpack(groups, members, heads_here, stages):
    rows = groups[0][0].shape[-2]
    counts = [len(group) for group in groups]
    messages = [message for group in groups for message in group]
    width = members * heads_here * HD
    return pl.pallas_call(
        functools.partial(unpack_kernel, members, heads_here, stages, counts),
        out_shape=[jax.ShapeDtypeStruct((rows, width), BF16)] * 3,
        in_specs=any_specs(len(messages)),
        out_specs=any_specs(3),
        scratch_shapes=[
            pltpu.VMEM((members, 3, rows, stage_heads * HD), BF16) for _, stage_heads in stages
        ]
        + [
            pltpu.SemaphoreType.DMA((len(stages), members)),
            pltpu.SemaphoreType.DMA((len(stages), members, 3)),
        ],
        compiler_params=params(56),
        cost_estimate=COST,
        name="unpack",
    )(*messages)


def exchange(messages, axis):
    count = len(messages)
    if count == 1:
        return [lax.all_to_all(messages[0], axis, split_axis=0, concat_axis=0, tiled=True)]
    return [
        lax.ppermute(message, axis, [(i, i ^ offset) for i in range(count)]) if offset else message
        for offset, message in zip(offsets_of(count), messages)
    ]


def turn_tables(lengths_row, total):
    positions = jnp.arange(total, dtype=jnp.int32)
    ends = jnp.cumsum(lengths_row)
    starts = ends - lengths_row
    begin = jnp.max(jnp.where(positions[:, None] >= starts[None, :], starts[None, :], 0), axis=1)
    half = HD // 2
    inverse = jnp.exp(-(jnp.arange(half, dtype=F32) * (2.0 / HD)) * math.log(10000.0))
    angles = inverse[:, None] * (positions - begin).astype(F32)[None, :]
    return jnp.cos(angles), jnp.sin(angles)


def shards(
    hidden,
    queries,
    key_states,
    value_states,
    attention_out,
    grad_out,
    lengths,
    down_query,
    up_query,
    down_value,
    up_value,
):
    rows = queries.shape[0]
    members = lax.axis_size("seq")
    packs = lax.axis_size("dp")
    total = rows * members
    heads_here = H // members
    stages = [(0, heads_here)]
    if heads_here > 1:
        stages = [(0, heads_here - LAST_HEADS), (heads_here - LAST_HEADS, LAST_HEADS)]
    sources = (queries, key_states, value_states, grad_out)
    me = lax.axis_index("seq")

    side_sources = (attention_out, grad_out, hidden, down_query, down_value)
    turns = turn_tables(lengths[0], total)
    beside = lax.ppermute(hidden, "seq", [(i, i ^ 1) for i in range(members)])
    packed = []
    for (first_head, stage_heads), whole in zip(stages, WHOLE_IN):
        extra = () if packed else side_sources
        held_back = sources
        if packed:
            held_back, _, beside = lax.optimization_barrier((sources, packed[0][0], beside))
        packed.append(
            list(pack(held_back, extra, members, heads_here, first_head, stage_heads, whole))
        )
    arrived = []
    home = []
    ups = []
    back = [None]
    planned = len(stages) == 2 and members == 8

    def after(value, stage, offsets):
        if not planned or not offsets:
            return value
        places = [offsets_of(members).index(offset) for offset in offsets]
        if len(home[stage]) == 1:
            places = [0]
        taken = tuple(home[stage][place] for place in places)
        value, taken = lax.optimization_barrier((value, taken))
        for place, message in zip(places, taken):
            home[stage][place] = message
        return value

    for index, (first_head, stage_heads) in enumerate(stages):
        arrived.append(exchange(packed[index], "seq"))
        if planned and index == 0:
            for place, before in CHAIN:
                packed[1][place], arrived[0][before] = lax.optimization_barrier(
                    (packed[1][place], arrived[0][before])
                )
        start = (me * heads_here + first_head) * HD
        up_here = tuple(
            lax.dynamic_slice_in_dim(up, start, stage_heads * HD, 1) for up in (up_query, up_value)
        )
        grads, back, up_terms = attention(
            lengths,
            up_here,
            turns,
            arrived[index],
            arrived[0],
            back[0],
            heads_here,
            first_head,
            stage_heads,
            members,
            rows,
            WHOLE_OUT[index],
        )
        back = list(back)
        home.append(list(grads) if index else exchange(grads, "seq"))
        ups.append(up_terms)
    home_early = not (planned and len(home[-1]) == 1)
    if len(home) > 1 and home_early:
        home[1] = exchange(home[1], "seq")

    def swap(value, offset):
        return lax.ppermute(value, "seq", [(i, i ^ offset) for i in range(members)])

    def planned_after(value, place):
        return after(after(value, 0, PLAN[place][0]), 1, PLAN[place][1])

    back = planned_after(list(back), 0)
    tiles = [
        swap(tile, offset) if offset else tile
        for offset, tile in zip(pair_offsets(members), back)
    ]
    own = planned_after(fold(tiles, ups), 1)
    if not home_early and LATE_OUT == -1:
        own, home[1][0] = lax.optimization_barrier((own, home[1][0]))
    other = planned_after(swap(own, 1), 2)
    if not home_early and LATE_OUT == 0:
        other, home[1][0] = lax.optimization_barrier((other, home[1][0]))
    pieces = list(down_terms(own, other, hidden, beside, members, packs))
    if not home_early and LATE_OUT == 1:
        pieces[0], home[1][0] = lax.optimization_barrier((pieces[0], home[1][0]))
    if not home_early:
        home[1] = exchange(home[1], "seq")
    pieces = exchange(pieces, "dp")
    down_cols = hidden.shape[1] // packs
    summed = planned_after(sum_packs(pieces, members // packs // 2, down_cols), 3)
    if members == 8:
        pieces = [swap(summed, offset) if offset else summed for offset in pair_offsets(members)]
    else:
        step = 2
        while step < members // 2:
            summed = summed + swap(summed, step)
            step *= 2
        pieces = [summed, swap(summed, step)]
    summed = planned_after(sum_chips(pieces), 4)
    down_query_grad, up_query_grad, down_value_grad, up_value_grad = finish(
        summed, swap(summed, 1), down_cols
    )
    grad_queries, grad_keys, value_gradients = unpack(home, members, heads_here, stages)
    return (
        grad_queries,
        grad_keys,
        value_gradients,
        down_query_grad,
        up_query_grad,
        down_value_grad,
        up_value_grad,
    )


def solution(mesh):
    tokens = P(("dp", "seq"), None)
    placed = (tokens,) * 6 + (P("dp", None),) + (P(),) * 4
    return jax.shard_map(
        shards,
        mesh=mesh,
        in_specs=placed,
        out_specs=(tokens,) * 3 + (P(None, "dp"),) * 4,
        check_vma=False,
    )
```

```python
import functools
import math

import jax
import jax.numpy as jnp
from jax import lax
from jax.experimental import pallas as pl
from jax.experimental.pallas import tpu as pltpu
from jax.sharding import PartitionSpec as P

H = 32
HD = 128
RANK = 8
ADAPTER_ALPHA = 16
SCALING = 1.0 / math.sqrt(HD)
LOG2E = 1.4426950408889634
BF16 = jnp.bfloat16
F32 = jnp.float32
NT = (((1,), (1,)), ((), ()))
MIB = 1024 * 1024
COST = pl.CostEstimate(flops=0, bytes_accessed=0, transcendentals=0)
ATTENTION_COST = pl.CostEstimate(flops=10**10, bytes_accessed=0, transcendentals=0)
LAST_HEADS = 2
LATE_OUT = 0
WHOLE_IN = (False, False)
WHOLE_OUT = (False, True)
ORDER = (6, 2, 4, 3, 5, 7, 1)
CHAIN = tuple((place, max(1, place - 3)) for place in range(1, 8))
PLAN = (
    ((6, 2, 4), ()),
    ((), ()),
    ((3, 5), ()),
    ((), ()),
    ((7, 1), (1,)),
)


def params(mebibytes):
    return pltpu.CompilerParams(vmem_limit_bytes=mebibytes * MIB)


def offsets_of(count):
    return (0,) + ORDER if count == 1 + len(ORDER) else tuple(range(count))


def pair_offsets(members):
    return [offset for offset in offsets_of(members) if offset % 2 == 0]


def part_of(refs, me, offset):
    if len(refs) == 1:
        return refs[0].at[me ^ offset]
    return refs[offsets_of(len(refs)).index(offset)]


def group_shapes(whole, members, shape, dtype):
    if whole:
        return [jax.ShapeDtypeStruct((members,) + shape, dtype)]
    return [jax.ShapeDtypeStruct(shape, dtype)] * members


def any_specs(count):
    return [pl.BlockSpec(memory_space=pl.ANY)] * count


def vmem_specs(count):
    return [pl.BlockSpec(memory_space=pltpu.VMEM)] * count


def dot_nt(left, right):
    return lax.dot_general(left, right, NT, preferred_element_type=F32)


def two_parts(value):
    high = value.astype(BF16)
    low = (value - high.astype(F32)).astype(BF16)
    return high, low


def three_parts(value):
    high, _ = two_parts(value)
    rest = value - high.astype(F32)
    middle, low = two_parts(rest)
    return high, middle, low


def side_rows(out, grad, hidden, downs):
    rows = out.shape[0]
    product = out.astype(F32) * grad.astype(F32)
    heads_at = lax.broadcasted_iota(jnp.int32, (H * HD, 128), 0) // HD
    lanes = lax.broadcasted_iota(jnp.int32, (H * HD, 128), 1)
    pick = jnp.where(heads_at == lanes, 1.0, 0.0).astype(BF16)
    split = jnp.concatenate(three_parts(product), axis=0)
    sums = jnp.dot(split, pick, preferred_element_type=F32)
    delta = (sums[:rows] + (sums[rows : 2 * rows] + sums[2 * rows :])).T[:H]
    return three_parts(delta), dot_nt(hidden, downs).T.astype(BF16)


def pack_kernel(members, heads_here, first_head, stage_heads, with_side, whole, *refs):
    refs = list(refs)
    sources = [refs.pop(0) for _ in range(4)]
    side_refs = [refs.pop(0) for _ in range(5 if with_side else 0)]
    messages = [refs.pop(0) for _ in range(1 if whole else members)]
    held, in_sems, out_sems = refs[:3]
    side_held, side_sems = refs[3:-1], refs[-1]
    me = lax.axis_index("seq")
    rows = sources[0].shape[0]
    reads = []
    for offset in range(members):
        target = me ^ offset
        for head in range(stage_heads):
            start = pl.multiple_of((target * heads_here + first_head + head) * HD, HD)
            for which in range(4):
                place = head * 4 + which
                reads.append(
                    pltpu.make_async_copy(
                        sources[which].at[:, pl.ds(start, HD)],
                        held.at[target, place * rows : (place + 1) * rows],
                        in_sems.at[offset, place],
                    )
                )
    bulk = 4 * stage_heads * rows

    def write(offset, low, count, sem):
        return pltpu.make_async_copy(
            held.at[me ^ offset, low : low + count],
            part_of(messages, me, offset).at[low : low + count],
            sem,
        )

    writes = [write(offset, 0, bulk, out_sems.at[0, offset]) for offset in range(members)]
    side_reads = [
        pltpu.make_async_copy(ref, there, side_sems.at[place])
        for place, (ref, there) in enumerate(zip(side_refs, side_held))
    ]
    for copy in reads + side_reads:
        copy.start()
    per_message = 4 * stage_heads
    for offset in range(members):
        for place in range(per_message):
            reads[offset * per_message + place].wait()
        writes[offset].start()
    if with_side:
        for copy in side_reads:
            copy.wait()
        out, grad, hidden, downq, downv = (there[...] for there in side_held)
        parts, lows = side_rows(out, grad, hidden, jnp.concatenate([downq, downv], axis=0))
        blank = jnp.zeros((16 - 3 * heads_here, rows), BF16)
        for member in range(members):
            here = slice(member * heads_here, (member + 1) * heads_here)
            held[member, bulk:] = jnp.concatenate(
                [part[here] for part in parts] + [blank, lows], axis=0
            )
        for offset in range(members):
            writes.append(write(offset, bulk, 32, out_sems.at[1, offset]))
            writes[-1].start()
    for copy in writes:
        copy.wait()


def pack(sources, side_sources, members, heads_here, first_head, stage_heads, whole):
    rows = sources[0].shape[0]
    shape = (4 * stage_heads * rows + (32 if side_sources else 0), HD)
    size = 2 * 4 * rows * stage_heads * HD * members * 2
    return pl.pallas_call(
        functools.partial(
            pack_kernel, members, heads_here, first_head, stage_heads, bool(side_sources), whole
        ),
        out_shape=group_shapes(whole, members, shape, BF16),
        in_specs=any_specs(4 + len(side_sources)),
        out_specs=any_specs(1 if whole else members),
        scratch_shapes=[
            pltpu.VMEM((members,) + shape, BF16),
            pltpu.SemaphoreType.DMA((members, 4 * stage_heads)),
            pltpu.SemaphoreType.DMA((2, members)),
        ]
        + [pltpu.VMEM(source.shape, BF16) for source in side_sources]
        + [pltpu.SemaphoreType.DMA((5,))],
        compiler_params=params(56),
        cost_estimate=COST,
        name="pack",
    )(*sources, *side_sources)


def begin_of(lengths_ref, positions):
    begin = jnp.int32(0) * positions
    start = jnp.int32(0)
    for index in range(lengths_ref.shape[1] - 1):
        start = start + lengths_ref[0, index]
        begin = jnp.where(positions >= start, start, begin)
    return begin


def attention_kernel(
    members,
    heads_here,
    first_head,
    stage_heads,
    counts,
    lengths_ref,
    upq_ref,
    upv_ref,
    cos_ref,
    sin_ref,
    *refs,
):
    refs = list(refs)
    messages, sides, outs, backs = [], [], [], []
    for group, count in zip((messages, sides), counts):
        group.extend(refs.pop(0) for _ in range(count))
    sides = sides or messages
    earlier_back = None if first_head == 0 else refs.pop(0)
    for group, count in zip((outs, backs), counts[2:]):
        group.extend(refs.pop(0) for _ in range(count))
    last = first_head + stage_heads == heads_here
    terms_ref = refs.pop(0)
    held, side_held, key_flip, grads, key_acc, value_acc, back_ref = refs[:7]
    in_sems, side_sems, out_sems = refs[7:]
    me = lax.axis_index("seq")
    side_low = sides[0].shape[-2] - 32
    rows = side_held.shape[1] // members
    total = rows * members
    block = min(256, total)
    reach = total // 2
    rows_of = [
        pl.ds(pl.multiple_of((me ^ offset) * rows, rows), rows) for offset in range(members)
    ]
    copies = []
    for offset in range(members):
        copies.append(
            pltpu.make_async_copy(
                part_of(messages, me, offset), held.at[me ^ offset], in_sems.at[offset]
            )
        )
        copies.append(
            pltpu.make_async_copy(
                part_of(sides, me, offset).at[side_low : side_low + 32],
                side_held.at[:, rows_of[offset]],
                side_sems.at[offset],
            )
        )
    for copy in copies:
        copy.start()
    key_acc[...] = jnp.zeros_like(key_acc)
    value_acc[...] = jnp.zeros_like(value_acc)
    terms_ref[...] = jnp.zeros_like(terms_ref)
    for copy in copies:
        copy.wait()
    columns = [slice(head * HD, (head + 1) * HD) for head in range(stage_heads)]

    def rows_at(place, low, count):
        first = low // rows
        taken = held[pl.ds(first, count // rows), place * rows : (place + 1) * rows, :]
        return taken.reshape(count, HD)

    for head in range(stage_heads):
        key_flip[head] = rows_at(4 * head + 1, 0, total).astype(F32).T.astype(BF16)

    def query_block(low, key_low, width):
        positions = low + lax.broadcasted_iota(jnp.int32, (1, block), 1)
        begin = begin_of(lengths_ref, positions)
        key_positions = key_low + lax.broadcasted_iota(jnp.int32, (width, block), 0)
        allowed = (key_positions >= begin) & (key_positions <= positions)
        bias = jnp.where(allowed, 0.0, -1e30).astype(F32)
        here = pl.ds(low, block)
        keys_here = pl.ds(key_low, width)
        cosine = cos_ref[:, here]
        sine = sin_ref[:, here]
        back_query = jnp.zeros((RANK, block), F32)
        parts = side_held[0:16, here].astype(F32)
        for head in range(stage_heads):
            cols = columns[head]
            query = rows_at(4 * head, low, block)
            grad = rows_at(4 * head + 3, low, block)
            scores = dot_nt(rows_at(4 * head + 1, key_low, width), query) + bias
            grad_prob = dot_nt(rows_at(4 * head + 2, key_low, width), grad)
            top = jnp.max(scores, axis=0, keepdims=True)
            weights = jnp.exp2((scores - top) * (SCALING * LOG2E))
            inverse = 1.0 / jnp.sum(weights, axis=0, keepdims=True)
            probs = weights * inverse
            row = first_head + head
            delta = sum(
                parts[place : place + 1] for place in range(row, 3 * heads_here, heads_here)
            )
            grad_score = (probs * (grad_prob - delta)).astype(BF16)
            value_acc[head, keys_here, :] += jnp.dot(
                probs.astype(BF16), grad, preferred_element_type=F32
            )
            key_acc[head, keys_here, :] += jnp.dot(grad_score, query, preferred_element_type=F32)
            flipped = SCALING * jnp.dot(
                key_flip[head, :, keys_here], grad_score, preferred_element_type=F32
            )
            grads[pl.ds(low // rows, block // rows), 0, :, cols] = (
                flipped.T.astype(BF16).reshape(block // rows, rows, HD)
            )
            rounded = flipped.astype(BF16).astype(F32)
            first = rounded[: HD // 2]
            second = rounded[HD // 2 :]
            before = jnp.concatenate(
                [first * cosine + second * sine, second * cosine - first * sine], axis=0
            ).astype(BF16)
            back_query += jnp.dot(upq_ref[:, cols], before, preferred_element_type=F32)
            terms_ref[0:RANK, cols] += dot_nt(side_held[16:24, here], before)
        back_ref[0:RANK, here] = back_query

    widths = [block + part * reach // 4 for part in range(5)]

    @pl.loop(0, total // block)
    def _(index):
        low = pl.multiple_of(index * block, block)
        needed = low + block - begin_of(lengths_ref, low)
        for place, width in enumerate(widths):
            fits = needed <= width
            if place:
                fits = fits & (needed > widths[place - 1])

            @pl.when(fits)
            def _(width=width):
                key_low = pl.multiple_of(jnp.maximum(low + block - width, 0), 128)
                query_block(low, key_low, width)

    back_value = jnp.zeros((RANK, total), F32)
    for head in range(stage_heads):
        cols = columns[head]
        grads[:, 1, :, cols] = (key_acc[head] * SCALING).astype(BF16).reshape(members, rows, HD)
        value_grad = value_acc[head].astype(BF16)
        grads[:, 2, :, cols] = value_grad.reshape(members, rows, HD)
        back_value += dot_nt(upv_ref[:, cols], value_grad)
        terms_ref[RANK : 2 * RANK, cols] = jnp.dot(
            side_held[24:32, :], value_grad, preferred_element_type=F32
        )
    back_ref[RANK : 2 * RANK, :] = back_value
    copies = [
        pltpu.make_async_copy(
            grads.at[me ^ offset], part_of(outs, me, offset), out_sems.at[offset]
        )
        for offset in range(members)
    ]
    for copy in copies:
        copy.start()
    back = back_ref[...]
    if earlier_back is not None:
        back = back + earlier_back[...]
    if last:
        back_ref[...] = back
        for out, offset in zip(backs, pair_offsets(members)):
            low = pl.multiple_of((me ^ offset) // 2 * 2 * rows, 2 * rows)
            out[...] = back_ref[:, pl.ds(low, 2 * rows)]
    else:
        backs[0][...] = back
    for copy in copies:
        copy.wait()


def attention(
    lengths,
    ups,
    turns,
    messages,
    sides,
    earlier_back,
    heads_here,
    first_head,
    stage_heads,
    members,
    rows,
    whole_out,
):
    total = rows * members
    width = stage_heads * HD
    last = first_head + stage_heads == heads_here
    out_shapes = group_shapes(whole_out, members, (3, rows, width), BF16)
    back_shapes = [jax.ShapeDtypeStruct((2 * RANK, total), F32)]
    if last:
        back_shapes = [jax.ShapeDtypeStruct((2 * RANK, 2 * rows), F32)] * (members // 2)
    earlier = [] if first_head == 0 else list(sides) + [earlier_back]
    counts = (len(messages), len(earlier[:-1]), len(out_shapes), len(back_shapes))
    results = pl.pallas_call(
        functools.partial(attention_kernel, members, heads_here, first_head, stage_heads, counts),
        out_shape=out_shapes + back_shapes + [jax.ShapeDtypeStruct((2 * RANK, width), F32)],
        in_specs=[pl.BlockSpec(memory_space=pltpu.SMEM)]
        + vmem_specs(4)
        + any_specs(len(messages))
        + (any_specs(len(sides)) + vmem_specs(1) if earlier else []),
        out_specs=any_specs(len(out_shapes)) + vmem_specs(len(back_shapes) + 1),
        scratch_shapes=[
            pltpu.VMEM((members,) + messages[0].shape[-2:], BF16),
            pltpu.VMEM((32, total), BF16),
            pltpu.VMEM((stage_heads, HD, total), BF16),
            pltpu.VMEM((members, 3, rows, width), BF16),
            pltpu.VMEM((stage_heads, total, HD), F32),
            pltpu.VMEM((stage_heads, total, HD), F32),
            pltpu.VMEM((2 * RANK, total), F32),
            pltpu.SemaphoreType.DMA((members,)),
            pltpu.SemaphoreType.DMA((members,)),
            pltpu.SemaphoreType.DMA((members,)),
        ],
        compiler_params=params(32),
        cost_estimate=ATTENTION_COST,
        name="attention",
    )(lengths, *ups, *turns, *messages, *earlier)
    split = len(out_shapes)
    return results[:split], results[split:-1], results[-1]


def small_call(kernel, out_shape, *operands, mebibytes=4, name="sum"):
    outs = len(out_shape) if isinstance(out_shape, list) else 1
    return pl.pallas_call(
        kernel,
        out_shape=out_shape,
        in_specs=vmem_specs(len(operands)),
        out_specs=vmem_specs(outs) if isinstance(out_shape, list) else vmem_specs(1)[0],
        compiler_params=params(mebibytes),
        cost_estimate=COST,
        name=name,
    )(*operands)


def total_of(refs):
    total = refs[0][...]
    for ref in refs[1:]:
        total = total + ref[...]
    return total


def fold(tiles, ups):
    def kernel(*refs):
        out = refs[-1]
        low = refs[0].shape[1]
        out[:, :low] = total_of(refs[: len(tiles)])
        for up in refs[len(tiles) : -1]:
            out[:, low : low + up.shape[1]] = up[...]
            low += up.shape[1]

    width = tiles[0].shape[1] + sum(up.shape[1] for up in ups)
    shape = jax.ShapeDtypeStruct((2 * RANK, width), F32)
    return small_call(kernel, shape, *tiles, *ups, name="fold")


def down_kernel(members, packs, own_ref, other_ref, hidden_ref, beside_ref, *refs):
    messages = refs[:packs]
    held, sems = refs[packs:]
    me = lax.axis_index("seq")
    pack_here = lax.axis_index("dp")
    first_core = me % 2 == 0
    rows = hidden_ref.shape[0]

    def half(value):
        return jnp.where(first_core, value[:RANK], value[RANK:])

    own, other = half(own_ref[...]), half(other_ref[...])
    back = own[:, : 2 * rows] + other[:, : 2 * rows]
    here = jnp.where(first_core, back[:, :rows], back[:, rows:]).astype(BF16)
    there = jnp.where(first_core, back[:, rows:], back[:, :rows]).astype(BF16)
    terms = jnp.dot(here, hidden_ref[...], preferred_element_type=F32) + jnp.dot(
        there, beside_ref[...], preferred_element_type=F32
    )
    own_up, other_up = own[:, 2 * rows :], other[:, 2 * rows :]
    ups = jnp.concatenate(
        [jnp.where(first_core, own_up, other_up), jnp.where(first_core, other_up, own_up)], axis=1
    )
    down_cols = terms.shape[1] // packs
    sharers = members // packs
    for target in range(packs):
        held[target, :, :down_cols] = terms[:, target * down_cols : (target + 1) * down_cols]
        held[target, :, down_cols:] = jnp.where(me // sharers == target, ups, 0.0)
    copies = [
        pltpu.make_async_copy(held.at[pack_here ^ offset], messages[offset], sems.at[offset])
        for offset in range(packs)
    ]
    for copy in copies:
        copy.start()
    for copy in copies:
        copy.wait()


def down_terms(own, other, hidden, beside, members, packs):
    rows = hidden.shape[0]
    width = hidden.shape[1] // packs + 2 * (own.shape[1] - 2 * rows)
    return pl.pallas_call(
        functools.partial(down_kernel, members, packs),
        out_shape=[jax.ShapeDtypeStruct((RANK, width), F32)] * packs,
        in_specs=vmem_specs(4),
        out_specs=any_specs(packs),
        scratch_shapes=[
            pltpu.VMEM((packs, RANK, width), F32),
            pltpu.SemaphoreType.DMA((packs,)),
        ],
        compiler_params=params(8),
        cost_estimate=COST,
        name="down_terms",
    )(own, other, hidden, beside)


def sum_packs(pieces, sharing_chips, down_cols):
    size = pieces[0].shape[1] - down_cols

    def kernel(*refs):
        out = refs[-1]
        me = lax.axis_index("seq")
        total = total_of(refs[:-1])
        out[:, :down_cols] = total[:, :down_cols]
        for place in range(sharing_chips):
            low = down_cols + place * size
            mine = (me // 2) % sharing_chips == place
            out[:, low : low + size] = jnp.where(mine, total[:, down_cols:], 0.0)

    shape = jax.ShapeDtypeStruct((RANK, down_cols + sharing_chips * size), F32)
    return small_call(kernel, shape, *pieces, name="sum_packs")


def sum_chips(pieces):
    def kernel(*refs):
        refs[-1][...] = total_of(refs[:-1]) * (ADAPTER_ALPHA / RANK)

    shape = jax.ShapeDtypeStruct(pieces[0].shape, F32)
    return small_call(kernel, shape, *pieces, name="sum_chips")


def finish(own, other, down_cols):
    def kernel(own_ref, other_ref, *outs):
        first_core = lax.axis_index("seq") % 2 == 0
        mine, beside = own_ref[...], other_ref[...]
        query = jnp.where(first_core, mine, beside)
        value = jnp.where(first_core, beside, mine)
        outs[0][...] = query[:, :down_cols]
        outs[1][...] = query[:, down_cols:]
        outs[2][...] = value[:, :down_cols]
        outs[3][...] = value[:, down_cols:]

    up_cols = own.shape[1] - down_cols
    shapes = [jax.ShapeDtypeStruct((RANK, cols), F32) for cols in (down_cols, up_cols)] * 2
    return small_call(kernel, shapes, own, other, name="finish")


def unpack_kernel(members, heads_here, stages, counts, *refs):
    count = sum(counts)
    groups = [refs[sum(counts[:i]) : sum(counts[: i + 1])] for i in range(len(counts))]
    outs = refs[count : count + 3]
    held = refs[count + 3 : count + 3 + len(stages)]
    in_sems, out_sems = refs[count + 3 + len(stages) :]
    me = lax.axis_index("seq")
    reads = []
    writes = []
    for stage, (first_head, stage_heads) in enumerate(stages):
        for offset in range(members):
            source = me ^ offset
            start = pl.multiple_of((source * heads_here + first_head) * HD, HD)
            reads.append(
                pltpu.make_async_copy(
                    part_of(groups[stage], me, offset),
                    held[stage].at[offset],
                    in_sems.at[stage, offset],
                )
            )
            writes.append(
                [
                    pltpu.make_async_copy(
                        held[stage].at[offset, which],
                        outs[which].at[:, pl.ds(start, stage_heads * HD)],
                        out_sems.at[stage, offset, which],
                    )
                    for which in range(3)
                ]
            )
    for copy in reads:
        copy.start()
    for copy, followers in zip(reads, writes):
        copy.wait()
        for follower in followers:
            follower.start()
    for followers in writes:
        for follower in followers:
            follower.wait()


def unpack(groups, members, heads_here, stages):
    rows = groups[0][0].shape[-2]
    counts = [len(group) for group in groups]
    messages = [message for group in groups for message in group]
    width = members * heads_here * HD
    return pl.pallas_call(
        functools.partial(unpack_kernel, members, heads_here, stages, counts),
        out_shape=[jax.ShapeDtypeStruct((rows, width), BF16)] * 3,
        in_specs=any_specs(len(messages)),
        out_specs=any_specs(3),
        scratch_shapes=[
            pltpu.VMEM((members, 3, rows, stage_heads * HD), BF16) for _, stage_heads in stages
        ]
        + [
            pltpu.SemaphoreType.DMA((len(stages), members)),
            pltpu.SemaphoreType.DMA((len(stages), members, 3)),
        ],
        compiler_params=params(56),
        cost_estimate=COST,
        name="unpack",
    )(*messages)


def exchange(messages, axis):
    count = len(messages)
    if count == 1:
        return [lax.all_to_all(messages[0], axis, split_axis=0, concat_axis=0, tiled=True)]
    return [
        lax.ppermute(message, axis, [(i, i ^ offset) for i in range(count)]) if offset else message
        for offset, message in zip(offsets_of(count), messages)
    ]


def turn_tables(lengths_row, total):
    positions = jnp.arange(total, dtype=jnp.int32)
    ends = jnp.cumsum(lengths_row)
    starts = ends - lengths_row
    begin = jnp.max(jnp.where(positions[:, None] >= starts[None, :], starts[None, :], 0), axis=1)
    half = HD // 2
    inverse = jnp.exp(-(jnp.arange(half, dtype=F32) * (2.0 / HD)) * math.log(10000.0))
    angles = inverse[:, None] * (positions - begin).astype(F32)[None, :]
    return jnp.cos(angles), jnp.sin(angles)


def shards(
    hidden,
    queries,
    key_states,
    value_states,
    attention_out,
    grad_out,
    lengths,
    down_query,
    up_query,
    down_value,
    up_value,
):
    rows = queries.shape[0]
    members = lax.axis_size("seq")
    packs = lax.axis_size("dp")
    total = rows * members
    heads_here = H // members
    stages = [(0, heads_here)]
    if heads_here > 1:
        stages = [(0, heads_here - LAST_HEADS), (heads_here - LAST_HEADS, LAST_HEADS)]
    sources = (queries, key_states, value_states, grad_out)
    me = lax.axis_index("seq")

    side_sources = (attention_out, grad_out, hidden, down_query, down_value)
    turns = turn_tables(lengths[0], total)
    beside = lax.ppermute(hidden, "seq", [(i, i ^ 1) for i in range(members)])
    packed = []
    for (first_head, stage_heads), whole in zip(stages, WHOLE_IN):
        extra = () if packed else side_sources
        held_back = sources
        if packed:
            held_back, _, beside = lax.optimization_barrier((sources, packed[0][0], beside))
        packed.append(
            list(pack(held_back, extra, members, heads_here, first_head, stage_heads, whole))
        )
    arrived = []
    home = []
    ups = []
    back = [None]
    planned = len(stages) == 2 and members == 8

    def after(value, stage, offsets):
        if not planned or not offsets:
            return value
        places = [offsets_of(members).index(offset) for offset in offsets]
        if len(home[stage]) == 1:
            places = [0]
        taken = tuple(home[stage][place] for place in places)
        value, taken = lax.optimization_barrier((value, taken))
        for place, message in zip(places, taken):
            home[stage][place] = message
        return value

    for index, (first_head, stage_heads) in enumerate(stages):
        arrived.append(exchange(packed[index], "seq"))
        if planned and index == 0:
            for place, before in CHAIN:
                packed[1][place], arrived[0][before] = lax.optimization_barrier(
                    (packed[1][place], arrived[0][before])
                )
        start = (me * heads_here + first_head) * HD
        up_here = tuple(
            lax.dynamic_slice_in_dim(up, start, stage_heads * HD, 1) for up in (up_query, up_value)
        )
        grads, back, up_terms = attention(
            lengths,
            up_here,
            turns,
            arrived[index],
            arrived[0],
            back[0],
            heads_here,
            first_head,
            stage_heads,
            members,
            rows,
            WHOLE_OUT[index],
        )
        back = list(back)
        home.append(list(grads) if index else exchange(grads, "seq"))
        ups.append(up_terms)
    home_early = not (planned and len(home[-1]) == 1)
    if len(home) > 1 and home_early:
        home[1] = exchange(home[1], "seq")

    def swap(value, offset):
        return lax.ppermute(value, "seq", [(i, i ^ offset) for i in range(members)])

    def planned_after(value, place):
        return after(after(value, 0, PLAN[place][0]), 1, PLAN[place][1])

    back = planned_after(list(back), 0)
    tiles = [
        swap(tile, offset) if offset else tile
        for offset, tile in zip(pair_offsets(members), back)
    ]
    own = planned_after(fold(tiles, ups), 1)
    if not home_early and LATE_OUT == -1:
        own, home[1][0] = lax.optimization_barrier((own, home[1][0]))
    other = planned_after(swap(own, 1), 2)
    if not home_early and LATE_OUT == 0:
        other, home[1][0] = lax.optimization_barrier((other, home[1][0]))
    pieces = list(down_terms(own, other, hidden, beside, members, packs))
    if not home_early and LATE_OUT == 1:
        pieces[0], home[1][0] = lax.optimization_barrier((pieces[0], home[1][0]))
    if not home_early:
        home[1] = exchange(home[1], "seq")
    pieces = exchange(pieces, "dp")
    down_cols = hidden.shape[1] // packs
    summed = planned_after(sum_packs(pieces, members // packs // 2, down_cols), 3)
    if members == 8:
        pieces = [swap(summed, offset) if offset else summed for offset in pair_offsets(members)]
    else:
        step = 2
        while step < members // 2:
            summed = summed + swap(summed, step)
            step *= 2
        pieces = [summed, swap(summed, step)]
    summed = planned_after(sum_chips(pieces), 4)
    down_query_grad, up_query_grad, down_value_grad, up_value_grad = finish(
        summed, swap(summed, 1), down_cols
    )
    grad_queries, grad_keys, value_gradients = unpack(home, members, heads_here, stages)
    return (
        grad_queries,
        grad_keys,
        value_gradients,
        down_query_grad,
        up_query_grad,
        down_value_grad,
        up_value_grad,
    )


def solution(mesh):
    tokens = P(("dp", "seq"), None)
    placed = (tokens,) * 6 + (P("dp", None),) + (P(),) * 4
    return jax.shard_map(
        shards,
        mesh=mesh,
        in_specs=placed,
        out_specs=(tokens,) * 3 + (P(None, "dp"),) * 4,
        check_vma=False,
    )
```

```python
import functools
import math

import jax
import jax.numpy as jnp
from jax import lax
from jax.experimental import pallas as pl
from jax.experimental.pallas import tpu as pltpu
from jax.sharding import PartitionSpec as P

H = 32
HD = 128
RANK = 8
ADAPTER_ALPHA = 16
SCALING = 1.0 / math.sqrt(HD)
LOG2E = 1.4426950408889634
BF16 = jnp.bfloat16
F32 = jnp.float32
NT = (((1,), (1,)), ((), ()))
MIB = 1024 * 1024
COST = pl.CostEstimate(flops=0, bytes_accessed=0, transcendentals=0)
ATTENTION_COST = pl.CostEstimate(flops=10**10, bytes_accessed=0, transcendentals=0)
LAST_HEADS = 2
LATE_OUT = 0
WHOLE_IN = (False, False)
WHOLE_OUT = (False, True)
ORDER = (6, 2, 4, 3, 5, 7, 1)
CHAIN = tuple((place, max(1, place - 3)) for place in range(1, 8))
PLAN = (
    ((6, 2, 4), ()),
    ((), ()),
    ((3, 5), ()),
    ((), ()),
    ((7, 1), (1,)),
)


def params(mebibytes):
    return pltpu.CompilerParams(vmem_limit_bytes=mebibytes * MIB)


def offsets_of(count):
    return (0,) + ORDER if count == 1 + len(ORDER) else tuple(range(count))


def pair_offsets(members):
    return [offset for offset in offsets_of(members) if offset % 2 == 0]


def part_of(refs, me, offset):
    if len(refs) == 1:
        return refs[0].at[me ^ offset]
    return refs[offsets_of(len(refs)).index(offset)]


def group_shapes(whole, members, shape, dtype):
    if whole:
        return [jax.ShapeDtypeStruct((members,) + shape, dtype)]
    return [jax.ShapeDtypeStruct(shape, dtype)] * members


def any_specs(count):
    return [pl.BlockSpec(memory_space=pl.ANY)] * count


def vmem_specs(count):
    return [pl.BlockSpec(memory_space=pltpu.VMEM)] * count


def dot_nt(left, right):
    return lax.dot_general(left, right, NT, preferred_element_type=F32)


def two_parts(value):
    high = value.astype(BF16)
    low = (value - high.astype(F32)).astype(BF16)
    return high, low


def three_parts(value):
    high, _ = two_parts(value)
    rest = value - high.astype(F32)
    middle, low = two_parts(rest)
    return high, middle, low


def side_rows(out, grad, hidden, downs):
    rows = out.shape[0]
    product = out.astype(F32) * grad.astype(F32)
    heads_at = lax.broadcasted_iota(jnp.int32, (H * HD, 128), 0) // HD
    lanes = lax.broadcasted_iota(jnp.int32, (H * HD, 128), 1)
    pick = jnp.where(heads_at == lanes, 1.0, 0.0).astype(BF16)
    split = jnp.concatenate(three_parts(product), axis=0)
    sums = jnp.dot(split, pick, preferred_element_type=F32)
    delta = (sums[:rows] + (sums[rows : 2 * rows] + sums[2 * rows :])).T[:H]
    return three_parts(delta), dot_nt(hidden, downs).T.astype(BF16)


def pack_kernel(members, heads_here, first_head, stage_heads, with_side, whole, *refs):
    refs = list(refs)
    sources = [refs.pop(0) for _ in range(4)]
    side_refs = [refs.pop(0) for _ in range(5 if with_side else 0)]
    messages = [refs.pop(0) for _ in range(1 if whole else members)]
    held, in_sems, out_sems = refs[:3]
    side_held, side_sems = refs[3:-1], refs[-1]
    me = lax.axis_index("seq")
    rows = sources[0].shape[0]
    reads = []
    for offset in range(members):
        target = me ^ offset
        for head in range(stage_heads):
            start = pl.multiple_of((target * heads_here + first_head + head) * HD, HD)
            for which in range(4):
                place = head * 4 + which
                reads.append(
                    pltpu.make_async_copy(
                        sources[which].at[:, pl.ds(start, HD)],
                        held.at[target, place * rows : (place + 1) * rows],
                        in_sems.at[offset, place],
                    )
                )
    bulk = 4 * stage_heads * rows

    def write(offset, low, count, sem):
        return pltpu.make_async_copy(
            held.at[me ^ offset, low : low + count],
            part_of(messages, me, offset).at[low : low + count],
            sem,
        )

    writes = [write(offset, 0, bulk, out_sems.at[0, offset]) for offset in range(members)]
    side_reads = [
        pltpu.make_async_copy(ref, there, side_sems.at[place])
        for place, (ref, there) in enumerate(zip(side_refs, side_held))
    ]
    for copy in reads + side_reads:
        copy.start()
    per_message = 4 * stage_heads
    for offset in range(members):
        for place in range(per_message):
            reads[offset * per_message + place].wait()
        writes[offset].start()
    if with_side:
        for copy in side_reads:
            copy.wait()
        out, grad, hidden, downq, downv = (there[...] for there in side_held)
        parts, lows = side_rows(out, grad, hidden, jnp.concatenate([downq, downv], axis=0))
        blank = jnp.zeros((16 - 3 * heads_here, rows), BF16)
        for member in range(members):
            here = slice(member * heads_here, (member + 1) * heads_here)
            held[member, bulk:] = jnp.concatenate(
                [part[here] for part in parts] + [blank, lows], axis=0
            )
        for offset in range(members):
            writes.append(write(offset, bulk, 32, out_sems.at[1, offset]))
            writes[-1].start()
    for copy in writes:
        copy.wait()


def pack(sources, side_sources, members, heads_here, first_head, stage_heads, whole):
    rows = sources[0].shape[0]
    shape = (4 * stage_heads * rows + (32 if side_sources else 0), HD)
    size = 2 * 4 * rows * stage_heads * HD * members * 2
    return pl.pallas_call(
        functools.partial(
            pack_kernel, members, heads_here, first_head, stage_heads, bool(side_sources), whole
        ),
        out_shape=group_shapes(whole, members, shape, BF16),
        in_specs=any_specs(4 + len(side_sources)),
        out_specs=any_specs(1 if whole else members),
        scratch_shapes=[
            pltpu.VMEM((members,) + shape, BF16),
            pltpu.SemaphoreType.DMA((members, 4 * stage_heads)),
            pltpu.SemaphoreType.DMA((2, members)),
        ]
        + [pltpu.VMEM(source.shape, BF16) for source in side_sources]
        + [pltpu.SemaphoreType.DMA((5,))],
        compiler_params=params(56),
        cost_estimate=COST,
        name="pack",
    )(*sources, *side_sources)


def begin_of(lengths_ref, positions):
    begin = jnp.int32(0) * positions
    start = jnp.int32(0)
    for index in range(lengths_ref.shape[1] - 1):
        start = start + lengths_ref[0, index]
        begin = jnp.where(positions >= start, start, begin)
    return begin


def attention_kernel(
    members,
    heads_here,
    first_head,
    stage_heads,
    counts,
    lengths_ref,
    upq_ref,
    upv_ref,
    cos_ref,
    sin_ref,
    *refs,
):
    refs = list(refs)
    messages, sides, outs, backs = [], [], [], []
    for group, count in zip((messages, sides), counts):
        group.extend(refs.pop(0) for _ in range(count))
    sides = sides or messages
    earlier_back = None if first_head == 0 else refs.pop(0)
    for group, count in zip((outs, backs), counts[2:]):
        group.extend(refs.pop(0) for _ in range(count))
    last = first_head + stage_heads == heads_here
    terms_ref = refs.pop(0)
    held, side_held, key_flip, grads, key_acc, value_acc, back_ref = refs[:7]
    in_sems, side_sems, out_sems = refs[7:]
    me = lax.axis_index("seq")
    side_low = sides[0].shape[-2] - 32
    rows = side_held.shape[1] // members
    total = rows * members
    block = min(256, total)
    reach = total // 2
    rows_of = [
        pl.ds(pl.multiple_of((me ^ offset) * rows, rows), rows) for offset in range(members)
    ]
    copies = []
    for offset in range(members):
        copies.append(
            pltpu.make_async_copy(
                part_of(messages, me, offset), held.at[me ^ offset], in_sems.at[offset]
            )
        )
        copies.append(
            pltpu.make_async_copy(
                part_of(sides, me, offset).at[side_low : side_low + 32],
                side_held.at[:, rows_of[offset]],
                side_sems.at[offset],
            )
        )
    for copy in copies:
        copy.start()
    key_acc[...] = jnp.zeros_like(key_acc)
    value_acc[...] = jnp.zeros_like(value_acc)
    terms_ref[...] = jnp.zeros_like(terms_ref)
    for copy in copies:
        copy.wait()
    columns = [slice(head * HD, (head + 1) * HD) for head in range(stage_heads)]

    def rows_at(place, low, count):
        first = low // rows
        taken = held[pl.ds(first, count // rows), place * rows : (place + 1) * rows, :]
        return taken.reshape(count, HD)

    for head in range(stage_heads):
        key_flip[head] = rows_at(4 * head + 1, 0, total).astype(F32).T.astype(BF16)

    def query_block(low, key_low, width):
        positions = low + lax.broadcasted_iota(jnp.int32, (1, block), 1)
        begin = begin_of(lengths_ref, positions)
        key_positions = key_low + lax.broadcasted_iota(jnp.int32, (width, block), 0)
        allowed = (key_positions >= begin) & (key_positions <= positions)
        bias = jnp.where(allowed, 0.0, -1e30).astype(F32)
        here = pl.ds(low, block)
        keys_here = pl.ds(key_low, width)
        cosine = cos_ref[:, here]
        sine = sin_ref[:, here]
        back_query = jnp.zeros((RANK, block), F32)
        parts = side_held[0:16, here].astype(F32)
        for head in range(stage_heads):
            cols = columns[head]
            query = rows_at(4 * head, low, block)
            grad = rows_at(4 * head + 3, low, block)
            scores = dot_nt(rows_at(4 * head + 1, key_low, width), query) + bias
            grad_prob = dot_nt(rows_at(4 * head + 2, key_low, width), grad)
            top = jnp.max(scores, axis=0, keepdims=True)
            weights = jnp.exp2((scores - top) * (SCALING * LOG2E))
            inverse = 1.0 / jnp.sum(weights, axis=0, keepdims=True)
            probs = weights * inverse
            row = first_head + head
            delta = sum(
                parts[place : place + 1] for place in range(row, 3 * heads_here, heads_here)
            )
            grad_score = (probs * (grad_prob - delta)).astype(BF16)
            value_acc[head, keys_here, :] += jnp.dot(
                probs.astype(BF16), grad, preferred_element_type=F32
            )
            key_acc[head, keys_here, :] += jnp.dot(grad_score, query, preferred_element_type=F32)
            flipped = SCALING * jnp.dot(
                key_flip[head, :, keys_here], grad_score, preferred_element_type=F32
            )
            grads[pl.ds(low // rows, block // rows), 0, :, cols] = (
                flipped.T.astype(BF16).reshape(block // rows, rows, HD)
            )
            rounded = flipped.astype(BF16).astype(F32)
            first = rounded[: HD // 2]
            second = rounded[HD // 2 :]
            before = jnp.concatenate(
                [first * cosine + second * sine, second * cosine - first * sine], axis=0
            ).astype(BF16)
            back_query += jnp.dot(upq_ref[:, cols], before, preferred_element_type=F32)
            terms_ref[0:RANK, cols] += dot_nt(side_held[16:24, here], before)
        back_ref[0:RANK, here] = back_query

    widths = [block + part * reach // 4 for part in range(5)]

    @pl.loop(0, total // block)
    def _(index):
        low = pl.multiple_of(index * block, block)
        needed = low + block - begin_of(lengths_ref, low)
        for place, width in enumerate(widths):
            fits = needed <= width
            if place:
                fits = fits & (needed > widths[place - 1])

            @pl.when(fits)
            def _(width=width):
                key_low = pl.multiple_of(jnp.maximum(low + block - width, 0), 128)
                query_block(low, key_low, width)

    back_value = jnp.zeros((RANK, total), F32)
    for head in range(stage_heads):
        cols = columns[head]
        grads[:, 1, :, cols] = (key_acc[head] * SCALING).astype(BF16).reshape(members, rows, HD)
        value_grad = value_acc[head].astype(BF16)
        grads[:, 2, :, cols] = value_grad.reshape(members, rows, HD)
        back_value += dot_nt(upv_ref[:, cols], value_grad)
        terms_ref[RANK : 2 * RANK, cols] = jnp.dot(
            side_held[24:32, :], value_grad, preferred_element_type=F32
        )
    back_ref[RANK : 2 * RANK, :] = back_value
    copies = [
        pltpu.make_async_copy(
            grads.at[me ^ offset], part_of(outs, me, offset), out_sems.at[offset]
        )
        for offset in range(members)
    ]
    for copy in copies:
        copy.start()
    back = back_ref[...]
    if earlier_back is not None:
        back = back + earlier_back[...]
    if last:
        back_ref[...] = back
        for out, offset in zip(backs, pair_offsets(members)):
            low = pl.multiple_of((me ^ offset) // 2 * 2 * rows, 2 * rows)
            out[...] = back_ref[:, pl.ds(low, 2 * rows)]
    else:
        backs[0][...] = back
    for copy in copies:
        copy.wait()


def attention(
    lengths,
    ups,
    turns,
    messages,
    sides,
    earlier_back,
    heads_here,
    first_head,
    stage_heads,
    members,
    rows,
    whole_out,
):
    total = rows * members
    width = stage_heads * HD
    last = first_head + stage_heads == heads_here
    out_shapes = group_shapes(whole_out, members, (3, rows, width), BF16)
    back_shapes = [jax.ShapeDtypeStruct((2 * RANK, total), F32)]
    if last:
        back_shapes = [jax.ShapeDtypeStruct((2 * RANK, 2 * rows), F32)] * (members // 2)
    earlier = [] if first_head == 0 else list(sides) + [earlier_back]
    counts = (len(messages), len(earlier[:-1]), len(out_shapes), len(back_shapes))
    results = pl.pallas_call(
        functools.partial(attention_kernel, members, heads_here, first_head, stage_heads, counts),
        out_shape=out_shapes + back_shapes + [jax.ShapeDtypeStruct((2 * RANK, width), F32)],
        in_specs=[pl.BlockSpec(memory_space=pltpu.SMEM)]
        + vmem_specs(4)
        + any_specs(len(messages))
        + (any_specs(len(sides)) + vmem_specs(1) if earlier else []),
        out_specs=any_specs(len(out_shapes)) + vmem_specs(len(back_shapes) + 1),
        scratch_shapes=[
            pltpu.VMEM((members,) + messages[0].shape[-2:], BF16),
            pltpu.VMEM((32, total), BF16),
            pltpu.VMEM((stage_heads, HD, total), BF16),
            pltpu.VMEM((members, 3, rows, width), BF16),
            pltpu.VMEM((stage_heads, total, HD), F32),
            pltpu.VMEM((stage_heads, total, HD), F32),
            pltpu.VMEM((2 * RANK, total), F32),
            pltpu.SemaphoreType.DMA((members,)),
            pltpu.SemaphoreType.DMA((members,)),
            pltpu.SemaphoreType.DMA((members,)),
        ],
        compiler_params=params(32),
        cost_estimate=ATTENTION_COST,
        name="attention",
    )(lengths, *ups, *turns, *messages, *earlier)
    split = len(out_shapes)
    return results[:split], results[split:-1], results[-1]


def small_call(kernel, out_shape, *operands, mebibytes=4, name="sum"):
    outs = len(out_shape) if isinstance(out_shape, list) else 1
    return pl.pallas_call(
        kernel,
        out_shape=out_shape,
        in_specs=vmem_specs(len(operands)),
        out_specs=vmem_specs(outs) if isinstance(out_shape, list) else vmem_specs(1)[0],
        compiler_params=params(mebibytes),
        cost_estimate=COST,
        name=name,
    )(*operands)


def total_of(refs):
    total = refs[0][...]
    for ref in refs[1:]:
        total = total + ref[...]
    return total


def fold(tiles, ups):
    def kernel(*refs):
        out = refs[-1]
        low = refs[0].shape[1]
        out[:, :low] = total_of(refs[: len(tiles)])
        for up in refs[len(tiles) : -1]:
            out[:, low : low + up.shape[1]] = up[...]
            low += up.shape[1]

    width = tiles[0].shape[1] + sum(up.shape[1] for up in ups)
    shape = jax.ShapeDtypeStruct((2 * RANK, width), F32)
    return small_call(kernel, shape, *tiles, *ups, name="fold")


def down_kernel(members, packs, own_ref, other_ref, hidden_ref, beside_ref, *refs):
    messages = refs[:packs]
    held, sems = refs[packs:]
    me = lax.axis_index("seq")
    pack_here = lax.axis_index("dp")
    first_core = me % 2 == 0
    rows = hidden_ref.shape[0]

    def half(value):
        return jnp.where(first_core, value[:RANK], value[RANK:])

    own, other = half(own_ref[...]), half(other_ref[...])
    back = own[:, : 2 * rows] + other[:, : 2 * rows]
    here = jnp.where(first_core, back[:, :rows], back[:, rows:]).astype(BF16)
    there = jnp.where(first_core, back[:, rows:], back[:, :rows]).astype(BF16)
    terms = jnp.dot(here, hidden_ref[...], preferred_element_type=F32) + jnp.dot(
        there, beside_ref[...], preferred_element_type=F32
    )
    own_up, other_up = own[:, 2 * rows :], other[:, 2 * rows :]
    ups = jnp.concatenate(
        [jnp.where(first_core, own_up, other_up), jnp.where(first_core, other_up, own_up)], axis=1
    )
    down_cols = terms.shape[1] // packs
    sharers = members // packs
    for target in range(packs):
        held[target, :, :down_cols] = terms[:, target * down_cols : (target + 1) * down_cols]
        held[target, :, down_cols:] = jnp.where(me // sharers == target, ups, 0.0)
    copies = [
        pltpu.make_async_copy(held.at[pack_here ^ offset], messages[offset], sems.at[offset])
        for offset in range(packs)
    ]
    for copy in copies:
        copy.start()
    for copy in copies:
        copy.wait()


def down_terms(own, other, hidden, beside, members, packs):
    rows = hidden.shape[0]
    width = hidden.shape[1] // packs + 2 * (own.shape[1] - 2 * rows)
    return pl.pallas_call(
        functools.partial(down_kernel, members, packs),
        out_shape=[jax.ShapeDtypeStruct((RANK, width), F32)] * packs,
        in_specs=vmem_specs(4),
        out_specs=any_specs(packs),
        scratch_shapes=[
            pltpu.VMEM((packs, RANK, width), F32),
            pltpu.SemaphoreType.DMA((packs,)),
        ],
        compiler_params=params(8),
        cost_estimate=COST,
        name="down_terms",
    )(own, other, hidden, beside)


def sum_packs(pieces, sharing_chips, down_cols):
    size = pieces[0].shape[1] - down_cols

    def kernel(*refs):
        out = refs[-1]
        me = lax.axis_index("seq")
        total = total_of(refs[:-1])
        out[:, :down_cols] = total[:, :down_cols]
        for place in range(sharing_chips):
            low = down_cols + place * size
            mine = (me // 2) % sharing_chips == place
            out[:, low : low + size] = jnp.where(mine, total[:, down_cols:], 0.0)

    shape = jax.ShapeDtypeStruct((RANK, down_cols + sharing_chips * size), F32)
    return small_call(kernel, shape, *pieces, name="sum_packs")


def sum_chips(pieces):
    def kernel(*refs):
        refs[-1][...] = total_of(refs[:-1]) * (ADAPTER_ALPHA / RANK)

    shape = jax.ShapeDtypeStruct(pieces[0].shape, F32)
    return small_call(kernel, shape, *pieces, name="sum_chips")


def finish(own, other, down_cols):
    def kernel(own_ref, other_ref, *outs):
        first_core = lax.axis_index("seq") % 2 == 0
        mine, beside = own_ref[...], other_ref[...]
        query = jnp.where(first_core, mine, beside)
        value = jnp.where(first_core, beside, mine)
        outs[0][...] = query[:, :down_cols]
        outs[1][...] = query[:, down_cols:]
        outs[2][...] = value[:, :down_cols]
        outs[3][...] = value[:, down_cols:]

    up_cols = own.shape[1] - down_cols
    shapes = [jax.ShapeDtypeStruct((RANK, cols), F32) for cols in (down_cols, up_cols)] * 2
    return small_call(kernel, shapes, own, other, name="finish")


def unpack_kernel(heads_here, stages, items, count, *refs):
    outs = refs[-6:-3]
    held, in_sems, out_sems = refs[-3:]
    me = lax.axis_index("seq")
    reads = []
    writes = []
    for slot, (index, stage, offset, whole) in enumerate(items):
        first_head, stage_heads = stages[stage]
        start = pl.multiple_of(((me ^ offset) * heads_here + first_head) * HD, HD)
        message = refs[index].at[me ^ offset] if whole else refs[index]
        reads.append(pltpu.make_async_copy(message, held.at[slot], in_sems.at[slot]))
        writes.append(
            [
                pltpu.make_async_copy(
                    held.at[slot, which],
                    outs[which].at[:, pl.ds(start, stage_heads * HD)],
                    out_sems.at[slot, which],
                )
                for which in range(3)
            ]
        )
    for copy in reads:
        copy.start()
    for copy, followers in zip(reads, writes):
        copy.wait()
        for follower in followers:
            follower.start()
    for followers in writes:
        for follower in followers:
            follower.wait()


def unpack(home, members, heads_here, stages, chosen, earlier):
    messages, items = [], []
    for stage, group in enumerate(home):
        for place, offset in enumerate(offsets_of(members)):
            whole = len(group) == 1
            if (stage, offset) in chosen:
                if not whole or place == 0:
                    messages.append(group[0 if whole else place])
                items.append((len(messages) - 1, stage, offset, whole))
    rows = messages[0].shape[-2]
    shape = jax.ShapeDtypeStruct((rows, members * heads_here * HD), BF16)
    count = len(messages)
    return pl.pallas_call(
        functools.partial(unpack_kernel, heads_here, stages, items, count),
        out_shape=[shape] * 3,
        in_specs=any_specs(count + len(earlier)),
        out_specs=any_specs(3),
        input_output_aliases={count + place: place for place in range(len(earlier))},
        scratch_shapes=[
            pltpu.VMEM((len(items), 3, rows, stages[0][1] * HD), BF16),
            pltpu.SemaphoreType.DMA((len(items),)),
            pltpu.SemaphoreType.DMA((len(items), 3)),
        ],
        compiler_params=params(56),
        cost_estimate=COST,
        name="unpack",
    )(*messages, *earlier)


def exchange(messages, axis):
    count = len(messages)
    if count == 1:
        return [lax.all_to_all(messages[0], axis, split_axis=0, concat_axis=0, tiled=True)]
    return [
        lax.ppermute(message, axis, [(i, i ^ offset) for i in range(count)]) if offset else message
        for offset, message in zip(offsets_of(count), messages)
    ]


def turn_tables(lengths_row, total):
    positions = jnp.arange(total, dtype=jnp.int32)
    ends = jnp.cumsum(lengths_row)
    starts = ends - lengths_row
    begin = jnp.max(jnp.where(positions[:, None] >= starts[None, :], starts[None, :], 0), axis=1)
    half = HD // 2
    inverse = jnp.exp(-(jnp.arange(half, dtype=F32) * (2.0 / HD)) * math.log(10000.0))
    angles = inverse[:, None] * (positions - begin).astype(F32)[None, :]
    return jnp.cos(angles), jnp.sin(angles)


def shards(
    hidden,
    queries,
    key_states,
    value_states,
    attention_out,
    grad_out,
    lengths,
    down_query,
    up_query,
    down_value,
    up_value,
):
    rows = queries.shape[0]
    members = lax.axis_size("seq")
    packs = lax.axis_size("dp")
    total = rows * members
    heads_here = H // members
    stages = [(0, heads_here)]
    if heads_here > 1:
        stages = [(0, heads_here - LAST_HEADS), (heads_here - LAST_HEADS, LAST_HEADS)]
    sources = (queries, key_states, value_states, grad_out)
    me = lax.axis_index("seq")

    side_sources = (attention_out, grad_out, hidden, down_query, down_value)
    turns = turn_tables(lengths[0], total)
    beside = lax.ppermute(hidden, "seq", [(i, i ^ 1) for i in range(members)])
    packed = []
    for (first_head, stage_heads), whole in zip(stages, WHOLE_IN):
        extra = () if packed else side_sources
        held_back = sources
        if packed:
            held_back, _, beside = lax.optimization_barrier((sources, packed[0][0], beside))
        packed.append(
            list(pack(held_back, extra, members, heads_here, first_head, stage_heads, whole))
        )
    arrived = []
    home = []
    ups = []
    back = [None]
    planned = len(stages) == 2 and members == 8

    def after(value, stage, offsets):
        if not planned or not offsets:
            return value
        places = [offsets_of(members).index(offset) for offset in offsets]
        if len(home[stage]) == 1:
            places = [0]
        taken = tuple(home[stage][place] for place in places)
        value, taken = lax.optimization_barrier((value, taken))
        for place, message in zip(places, taken):
            home[stage][place] = message
        return value

    for index, (first_head, stage_heads) in enumerate(stages):
        arrived.append(exchange(packed[index], "seq"))
        if planned and index == 0:
            for place, before in CHAIN:
                packed[1][place], arrived[0][before] = lax.optimization_barrier(
                    (packed[1][place], arrived[0][before])
                )
        start = (me * heads_here + first_head) * HD
        up_here = tuple(
            lax.dynamic_slice_in_dim(up, start, stage_heads * HD, 1) for up in (up_query, up_value)
        )
        grads, back, up_terms = attention(
            lengths,
            up_here,
            turns,
            arrived[index],
            arrived[0],
            back[0],
            heads_here,
            first_head,
            stage_heads,
            members,
            rows,
            WHOLE_OUT[index],
        )
        back = list(back)
        home.append(list(grads) if index else exchange(grads, "seq"))
        ups.append(up_terms)
    home_early = not (planned and len(home[-1]) == 1)
    if len(home) > 1 and home_early:
        home[1] = exchange(home[1], "seq")

    def swap(value, offset):
        return lax.ppermute(value, "seq", [(i, i ^ offset) for i in range(members)])

    def planned_after(value, place):
        return after(after(value, 0, PLAN[place][0]), 1, PLAN[place][1])

    back = planned_after(list(back), 0)
    tiles = [
        swap(tile, offset) if offset else tile
        for offset, tile in zip(pair_offsets(members), back)
    ]
    own = planned_after(fold(tiles, ups), 1)
    if not home_early and LATE_OUT == -1:
        own, home[1][0] = lax.optimization_barrier((own, home[1][0]))
    other = planned_after(swap(own, 1), 2)
    if not home_early and LATE_OUT == 0:
        other, home[1][0] = lax.optimization_barrier((other, home[1][0]))
    pieces = list(down_terms(own, other, hidden, beside, members, packs))
    if not home_early and LATE_OUT == 1:
        pieces[0], home[1][0] = lax.optimization_barrier((pieces[0], home[1][0]))
    if not home_early:
        home[1] = exchange(home[1], "seq")
    pieces = exchange(pieces, "dp")
    down_cols = hidden.shape[1] // packs
    summed = planned_after(sum_packs(pieces, members // packs // 2, down_cols), 3)
    if members == 8:
        pieces = [swap(summed, offset) if offset else summed for offset in pair_offsets(members)]
    else:
        step = 2
        while step < members // 2:
            summed = summed + swap(summed, step)
            step *= 2
        pieces = [summed, swap(summed, step)]
    everything = [(stage, offset) for stage in range(len(stages)) for offset in range(members)]
    early, earlier = [], ()
    if planned:
        early = [(0, offset) for offset in (0, 6, 2, 4, 3, 5)]
        earlier = tuple(unpack(home, members, heads_here, stages, early, ()))
        pieces, earlier = lax.optimization_barrier((pieces, earlier))
    summed = planned_after(sum_chips(pieces), 4)
    down_query_grad, up_query_grad, down_value_grad, up_value_grad = finish(
        summed, swap(summed, 1), down_cols
    )
    grad_queries, grad_keys, value_gradients = unpack(
        home, members, heads_here, stages, [at for at in everything if at not in early], earlier
    )
    return (
        grad_queries,
        grad_keys,
        value_gradients,
        down_query_grad,
        up_query_grad,
        down_value_grad,
        up_value_grad,
    )


def solution(mesh):
    tokens = P(("dp", "seq"), None)
    placed = (tokens,) * 6 + (P("dp", None),) + (P(),) * 4
    return jax.shard_map(
        shards,
        mesh=mesh,
        in_specs=placed,
        out_specs=(tokens,) * 3 + (P(None, "dp"),) * 4,
        check_vma=False,
    )
```
